128 devices in a mesh: col: 32 (over x, y, core), rank: 4 (over z).
Axes of the slice: x: 4, y: 4, z: 4, core: 2. Of those that a mesh axis runs over, the one named last changes fastest.
Arguments:
- coefficients: bfloat16 [16, 32, 64, 16384], P(None, None, None, ('col', 'rank')), may hold values from -6 to 6
- v_factors: bfloat16 [32, 64, 16384], P(None, None, ('col', 'rank')), may hold values from -0.25 to 0.25
- transfer: bfloat16 [3, 32, 32, 64, 128], P(None, None, 'col'), may hold values from -0.75 to 0.75
- u_factors: bfloat16 [32, 64, 16384], P(None, None, ('col', 'rank')), may hold values from -0.75 to 0.75
- orders: int32 [32], replicated, may hold values from 0 to 16383, as said below
- ranks: int32 [32], replicated, may hold values from 16 to 64
Outputs:
- transformed: bfloat16 [16, 32, 64, 16384], P(None, None, None, ('col', 'rank'))
The draws below stay inside these ranges and needn't reach their ends.
Inputs may be any that keep to these rules, and one draw needn't show every extreme that they name: `orders`: distinct and increasing.
All inputs are finite; a program needn't handle non-finite values.
Results may differ from the reference program's by a relative error of at most 0.007.
Values may be sent and summed in bfloat16 or wider, within the bound.
A program may use at most 128 MiB of HBM per device.

```python
import jax
import jax.numpy as jnp
from jax import lax

NDEG = 16384
ORDERS = 32
FIELDS = 64
RANK = 64
BATCHES = 16
LEVELS = 3
NBLOCKS = 32
N_COL = 32


def draw_orders(key, part):
    key = jax.random.fold_in(key, 11)
    stride = NDEG // ORDERS
    offsets = jax.random.randint(key, (ORDERS,), 0, stride, dtype=jnp.int32)
    picked = jnp.arange(ORDERS, dtype=jnp.int32) * stride + offsets
    picked = picked.at[0].set(0)
    picked = picked.at[ORDERS - 1].set(NDEG - 1)
    return picked


def draw_ranks(key, part):
    key = jax.random.fold_in(key, 23)
    first, second = jax.random.split(key)
    values = jax.random.randint(first, (ORDERS,), RANK // 4, RANK + 1, dtype=jnp.int32)
    shuffled = jax.random.permutation(second, ORDERS)
    values = values.at[shuffled[0]].set(RANK)
    values = values.at[shuffled[1]].set(RANK // 4)
    return values


def levels(stream_key, dims, pieces, smallest, largest):
    loudness = 1.0
    for axis_at, blocks in pieces:
        heights = jax.random.uniform(jax.random.fold_in(jax.random.fold_in(stream_key, 6), axis_at), (blocks,), jnp.float32, smallest / len(pieces), largest / len(pieces))
        loudness = loudness * jnp.repeat(jnp.exp(heights), dims[axis_at] // blocks).reshape((-1,) + (1,) * (len(dims) - 1 - axis_at))
    return loudness


def bell_draw(key, dims, scale, reach, cuts=(), held_as=jnp.bfloat16):
    drawn = jax.random.normal(key, dims, jnp.float32) * scale
    if len(cuts) > 0:
        drawn = levels(key, dims, cuts, -0.22, 0.18) * drawn
    return jnp.clip(drawn, min=-reach, max=reach).astype(held_as)


def setup_inputs(seed: int = 0) -> dict:
    keys = jax.random.split(jax.random.key(seed), 7)
    coefficients = bell_draw(keys[0], (BATCHES, ORDERS, FIELDS, NDEG), 1.0, 6.0, ((3, 128),))
    v_factors = bell_draw(keys[1], (ORDERS, RANK, NDEG), (NDEG // N_COL) ** -0.5, 0.25, ((2, 128),))
    transfer = bell_draw(keys[2], (LEVELS, ORDERS, NBLOCKS, RANK, 2 * RANK), RANK ** -0.5, 0.75, ((2, 32),))
    u_factors = bell_draw(keys[3], (ORDERS, RANK, NDEG), RANK ** -0.5, 0.75, ((2, 128),))
    orders = draw_orders(jax.random.fold_in(keys[6], 71), 0)
    ranks = draw_ranks(jax.random.fold_in(keys[6], 71), 0)
    return dict(coefficients=coefficients, v_factors=v_factors, transfer=transfer, u_factors=u_factors, orders=orders, ranks=ranks)


def reference(coefficients, v_factors, transfer, u_factors, orders, ranks):
    width = NDEG // N_COL
    degree = jnp.arange(NDEG, dtype=jnp.int32)
    input_mask = (degree[None, :] >= orders[:, None]).astype(jnp.bfloat16)
    keep_mask = (jnp.arange(RANK, dtype=jnp.int32)[None, :] < ranks[:, None]).astype(jnp.float32)
    nbits = N_COL.bit_length() - 1
    v_grid = v_factors.astype(jnp.float32).reshape(ORDERS, RANK, N_COL, width)
    u_grid = u_factors.astype(jnp.float32).reshape(ORDERS, RANK, N_COL, width)
    maps = transfer.astype(jnp.float32)

    def one_batch(fields_now):
        fields_now = fields_now * input_mask[:, None, :]
        grid = fields_now.astype(jnp.float32).reshape(ORDERS, FIELDS, N_COL, width)
        leaf = jnp.einsum("ofcw,okcw->ofck", grid, v_grid)
        state = (leaf * keep_mask[:, None, None, :]).astype(jnp.bfloat16)
        for layer_index in range(LEVELS):
            stride = 1 << (nbits - 1 - layer_index)
            grouped = state.reshape(ORDERS, FIELDS, N_COL // (2 * stride), 2, stride, RANK)
            partner = jnp.flip(grouped, axis=3).reshape(ORDERS, FIELDS, N_COL, RANK)
            stacked = jnp.concatenate([state, partner], axis=3).astype(jnp.float32)
            mixed = jnp.einsum("ofcj,ockj->ofck", stacked, maps[layer_index])
            state = (mixed * keep_mask[:, None, None, :]).astype(jnp.bfloat16)
        result = jnp.einsum("ofck,okcw->ofcw", state.astype(jnp.float32), u_grid)
        return result.reshape(ORDERS, FIELDS, NDEG).astype(jnp.bfloat16)

    return lax.map(one_batch, coefficients)
```

```python
import functools

import jax
import jax.numpy as jnp
from jax import lax
from jax.experimental import pallas as pl
from jax.experimental.pallas import tpu as pltpu
from jax.sharding import PartitionSpec as P

MESH = pl.DeviceIdType.MESH
BF16, F32, I32 = jnp.bfloat16, jnp.float32, jnp.int32
QUAD = 4
LAGS = (0, 2, 4, 6, 8, 9, 11, 13)


def dot(a, b, dims=((1,), (0,))):
    return lax.dot_general(a, b, (dims, ((), ())), preferred_element_type=F32)


def spots(plan, g):
    first = [plan[1, QUAD * g + i] for i in range(QUAD)]
    rank = [plan[2, QUAD * g + i] for i in range(QUAD)]
    return first, rank, first[QUAD - 1] + rank[QUAD - 1]


def placing(plan, g, rows, width):
    first, rank, _ = spots(plan, g)
    lane = lax.broadcasted_iota(I32, (1, QUAD * width), 1)
    target = jnp.full((1, QUAD * width), -1, I32)
    for i in range(QUAD):
        k = lane - i * width
        here = (k >= 0) & (k < rank[i])
        target = jnp.where(here, first[i] + k, target)
    row = lax.broadcasted_iota(I32, (rows, QUAD * width), 0)
    return jnp.where(row == target, 1.0, 0.0).astype(BF16)


def order_of(plan, g, index):
    first, _, _ = spots(plan, g)
    seg = jnp.zeros(index.shape, I32)
    for i in range(1, QUAD):
        seg = seg + jnp.where(index >= first[i], 1, 0)
    return seg


def mixing(rows, levels, lags, plan, x, v, t, out, a, place, maps, far, far_in, near, near_in, summed, summed_in,
           keep_next, keep_own, state, state_in, done, send, recv, out_sem):
    col, z = lax.axis_index("col"), lax.axis_index("rank")
    width = v.shape[1]
    chunks = out.shape[0]

    def flipped(bit):
        return col + bit - 2 * bit * lax.rem(lax.div(col, bit), 2)

    def at(step):
        return lax.rem(z + step, 4)

    n_col = lax.axis_size("col")
    partners = [(flipped(n_col >> (l + 1)), z) for l in range(levels)]

    barrier = pltpu.get_barrier_semaphore()
    for peer in [(col, at(1)), (col, at(3))] + partners:
        pl.semaphore_signal(barrier, inc=1, device_id=peer, device_id_type=MESH)
    pl.semaphore_wait(barrier, 2 + levels)

    def remote(kind, j, src, dst, peer):
        return pltpu.make_async_remote_copy(
            src_ref=src, dst_ref=dst, send_sem=send.at[kind, j], recv_sem=recv.at[kind, j],
            device_id=peer, device_id_type=MESH)

    FAR, NEAR, SUM, AHEAD, BACK, ON, LEVEL = 0, 1, 2, 3, 4, 5, 6

    def sides(j):
        h = lax.rem(j, 2)
        return at(1 + 2 * h), at(3 - 2 * h), at(2)

    def far_copy(j):
        ahead, _, _ = sides(j)
        return remote(FAR, j, far.at[j], far_in.at[j], (col, ahead))

    def near_copy(j):
        _, back, _ = sides(j)
        return remote(NEAR, j, near.at[j], near_in.at[j], (col, back))

    def sum_copy(j):
        ahead, _, _ = sides(j)
        return remote(SUM, j, summed.at[j], summed_in.at[j], (col, ahead))

    def level_copy(l, j):
        return remote(LEVEL + l, j, state.at[l, j], state_in.at[l, j], partners[l])

    def ahead_copy(j, q):
        ahead, _, _ = sides(j)
        return remote(AHEAD, j, done.at[j, q], done.at[j, q], (col, ahead))

    def back_copy(j, q):
        _, back, _ = sides(j)
        return remote(BACK, j, done.at[j, q], done.at[j, q], (col, back))

    def on_copy(j, q):
        ahead, _, _ = sides(j)
        return remote(ON, j, done.at[j, q], done.at[j, q], (col, ahead))

    def out_copy(j):
        return pltpu.make_async_copy(done.at[j], out.at[j], out_sem.at[j])

    def leaf(j):
        g, h = lax.div(j, 2), lax.rem(j, 2)
        ahead, back, across = sides(j)

        @pl.when(h == 0)
        def _():
            p = placing(plan, g, rows, width)
            place[...] = p
            degree = (col * 4 + z) * 128 + lax.broadcasted_iota(I32, (1, 128), 1)
            for i in range(QUAD):
                o = plan[0, QUAD * g + i]
                picked = dot(p[:, i * width:(i + 1) * width], v[o])
                kept = jnp.where(degree >= plan[3, QUAD * g + i], picked, 0.0)
                a[:, i * 128:(i + 1) * 128] = kept.astype(BF16)

        def fields(q):
            parts = []
            for b in range(2):
                batch = 4 * q + 2 * h + b
                parts.append(jnp.concatenate([x[batch, plan[0, QUAD * g + i]] for i in range(QUAD)], axis=1))
            return jnp.concatenate(parts, axis=0)

        sent = dot(a[...], jnp.concatenate([fields(across), fields(back)], axis=0), ((1,), (1,)))
        far[j] = sent[:, :128].astype(BF16)
        near[j] = sent[:, 128:].astype(BF16)
        far_copy(j).start()
        near_copy(j).start()
        kept = dot(a[...], jnp.concatenate([fields(ahead), fields(z)], axis=0), ((1,), (1,)))
        keep_next[j] = kept[:, :128]
        keep_own[j] = kept[:, 128:]

        @pl.when(h == 1)
        def _():
            _, _, filled = spots(plan, g)
            first, _, _ = spots(plan, g)
            lane = lax.broadcasted_iota(I32, (1, rows), 1)
            seg = order_of(plan, g, lane)
            k = lane
            for i in range(1, QUAD):
                k = jnp.where(seg == i, lane - first[i], k)
            k = jnp.where(lane < filled, k, -1000)
            j_row = lax.broadcasted_iota(I32, (2 * width, rows), 0)
            pick_own = jnp.where(j_row == k, 1.0, 0.0).astype(BF16)
            pick_partner = jnp.where(j_row - width == k, 1.0, 0.0).astype(BF16)
            row = lax.broadcasted_iota(I32, (rows, rows), 0)
            same = jnp.where(order_of(plan, g, row) == seg, 1.0, 0.0)
            p = place[...]
            for l in range(levels):
                stack = jnp.concatenate([t[l, plan[0, QUAD * g + i], 0] for i in range(QUAD)], axis=0)
                packed = dot(p, stack).astype(BF16)
                maps[l, g, 0] = (dot(packed, pick_own) * same).astype(BF16)
                maps[l, g, 1] = (dot(packed, pick_partner) * same).astype(BF16)

    def pass_on(j):
        far_copy(j).wait_recv()
        summed[j] = (keep_next[j] + far_in[j].astype(F32)).astype(BF16)
        sum_copy(j).start()

    def first_state(j):
        near_copy(j).wait_recv()
        sum_copy(j).wait_recv()
        total = keep_own[j] + near_in[j].astype(F32) + summed_in[j].astype(F32)
        state[0, j] = total.astype(BF16)
        level_copy(0, j).start()

    def mix(l, j):
        g = lax.div(j, 2)
        level_copy(l, j).wait_recv()
        new = dot(maps[l, g, 0], state[l, j]) + dot(maps[l, g, 1], state_in[l, j])
        return new.astype(BF16)

    def level(l, j):
        state[l + 1, j] = mix(l, j)
        level_copy(l + 1, j).start()

    def last_level(j):
        done[j, z] = mix(levels - 1, j)
        ahead_copy(j, z).start()
        back_copy(j, z).start()

    def hand_on(j):
        _, back, _ = sides(j)
        ahead_copy(j, back).wait_recv()
        on_copy(j, back).start()

    def finish(j):
        ahead, _, across = sides(j)
        back_copy(j, ahead).wait_recv()
        on_copy(j, across).wait_recv()
        out_copy(j).start()

    stages = [leaf, pass_on, first_state]
    stages += [functools.partial(level, l) for l in range(levels - 1)]
    stages += [last_level, hand_on, finish]

    def step(s, carry):
        for lag, stage in zip(lags, stages, strict=True):
            j = s - lag

            @pl.when((j >= 0) & (j < chunks))
            def _(stage=stage, j=j):
                stage(j)

        return carry

    lax.fori_loop(0, chunks + max(lags), step, 0)

    def settle(j, carry):
        _, back, _ = sides(j)
        far_copy(j).wait_send()
        near_copy(j).wait_send()
        sum_copy(j).wait_send()
        for l in range(levels):
            level_copy(l, j).wait_send()
        ahead_copy(j, z).wait_send()
        back_copy(j, z).wait_send()
        on_copy(j, back).wait_send()
        out_copy(j).wait()
        return carry

    lax.fori_loop(0, chunks, settle, 0)


def mixed(rows, cid, plan, x, v, t):
    levels, groups = t.shape[0], x.shape[1] // QUAD
    chunks = 2 * groups
    chunk = (chunks, rows, 128)
    kinds = 6 + levels
    vmem, smem, anywhere = (pl.BlockSpec(memory_space=m) for m in (pltpu.VMEM, pltpu.SMEM, pl.ANY))
    return pl.pallas_call(
        functools.partial(mixing, rows, levels, LAGS),
        out_shape=jax.ShapeDtypeStruct((chunks, 4, rows, 128), BF16),
        in_specs=[smem, vmem, vmem, vmem],
        out_specs=anywhere,
        scratch_shapes=[
            pltpu.VMEM((rows, QUAD * 128), BF16),
            pltpu.VMEM((rows, QUAD * v.shape[1]), BF16),
            pltpu.VMEM((levels, groups, 2, rows, rows), BF16),
            pltpu.VMEM(chunk, BF16), pltpu.VMEM(chunk, BF16),
            pltpu.VMEM(chunk, BF16), pltpu.VMEM(chunk, BF16),
            pltpu.VMEM(chunk, BF16), pltpu.VMEM(chunk, BF16),
            pltpu.VMEM(chunk, F32), pltpu.VMEM(chunk, F32),
            pltpu.VMEM((levels, *chunk), BF16), pltpu.VMEM((levels, *chunk), BF16),
            pltpu.VMEM((chunks, 4, rows, 128), BF16),
            pltpu.SemaphoreType.DMA((kinds, chunks)),
            pltpu.SemaphoreType.DMA((kinds, chunks)),
            pltpu.SemaphoreType.DMA((chunks,)),
        ],
        compiler_params=pltpu.CompilerParams(
            collective_id=cid, has_side_effects=True, vmem_limit_bytes=58 * 2**20),
        cost_estimate=pl.CostEstimate(flops=10**9, bytes_accessed=16 * 2**20, transcendentals=0),
    )(plan, x, v, t)


def writing(rows, plan, s, u, out, buf, sem):
    g, groups = pl.program_id(0), pl.num_programs(0)
    slot = lax.rem(g, 2)
    width = u.shape[1]

    def copies(group, slot):
        return [pltpu.make_async_copy(buf.at[slot, i], out.at[:, plan[0, QUAD * group + i]], sem.at[slot, i])
                for i in range(QUAD)]

    p = placing(plan, g, rows, width)
    packed = [dot(p[:, i * width:(i + 1) * width], u[plan[0, QUAD * g + i]]).astype(BF16) for i in range(QUAD)]
    packed = jnp.concatenate(packed, axis=1)

    @pl.when(g >= 2)
    def _():
        for c in copies(g - 2, slot):
            c.wait()

    for h in range(2):
        for q in range(4):
            points = dot(s[h, q], packed, ((0,), (0,))).astype(BF16)
            for i in range(QUAD):
                for b in range(2):
                    buf[slot, i, 4 * q + 2 * h + b] = points[b * 64:(b + 1) * 64, i * 128:(i + 1) * 128]
    for c in copies(g, slot):
        c.start()

    @pl.when(g == groups - 1)
    def _():
        for c in copies(g - 1, 1 - slot) + copies(g, slot):
            c.wait()


def written(rows, plan, s, u, shape):
    groups = shape[1] // QUAD
    return pl.pallas_call(
        functools.partial(writing, rows),
        out_shape=jax.ShapeDtypeStruct(shape, BF16),
        grid_spec=pltpu.PrefetchScalarGridSpec(
            num_scalar_prefetch=1,
            grid=(groups,),
            in_specs=[pl.BlockSpec((2, 4, rows, 128), lambda g, plan: (g, 0, 0, 0)),
                      pl.BlockSpec(memory_space=pltpu.VMEM)],
            out_specs=pl.BlockSpec(memory_space=pl.ANY),
            scratch_shapes=[pltpu.VMEM((2, QUAD, shape[0], shape[2], shape[3]), BF16),
                            pltpu.SemaphoreType.DMA((2, QUAD))],
        ),
        compiler_params=pltpu.CompilerParams(vmem_limit_bytes=48 * 2**20),
    )(plan, s, u)


def shards(coefficients, v_factors, transfer, u_factors, orders, ranks):
    count = orders.shape[0]
    rows = QUAD * v_factors.shape[1]
    perm = lax.iota(I32, count)
    place = ranks.reshape(-1, QUAD)
    first = (jnp.cumsum(place, axis=1) - place).reshape(count)
    plan = jnp.stack([perm, first, ranks, orders])
    s = mixed(rows, 1, plan, coefficients, v_factors, transfer)
    return written(rows, plan, s, u_factors, coefficients.shape)


def solution(mesh):
    placed = (
        P(None, None, None, ("col", "rank")),
        P(None, None, ("col", "rank")),
        P(None, None, "col", None, None),
        P(None, None, ("col", "rank")),
        P(),
        P(),
    )
    return jax.shard_map(
        shards,
        mesh=mesh,
        in_specs=placed,
        out_specs=P(None, None, None, ("col", "rank")),
        check_vma=False,
    )
```

```python
import functools

import jax
import jax.numpy as jnp
from jax import lax
from jax.experimental import pallas as pl
from jax.experimental.pallas import tpu as pltpu
from jax.sharding import PartitionSpec as P

MESH = pl.DeviceIdType.MESH
BF16, F32, I32 = jnp.bfloat16, jnp.float32, jnp.int32
QUAD = 4
LAGS = (0, 2, 4, 6, 8, 9, 11, 13)
PARTS = (10, 11, 12, 16)


def dot(a, b, dims=((1,), (0,))):
    return lax.dot_general(a, b, (dims, ((), ())), preferred_element_type=F32)


def spots(plan, g):
    first = [plan[1, QUAD * g + i] for i in range(QUAD)]
    rank = [plan[2, QUAD * g + i] for i in range(QUAD)]
    return first, rank, first[QUAD - 1] + rank[QUAD - 1]


def placing(plan, g, rows, width):
    first, rank, _ = spots(plan, g)
    lane = lax.broadcasted_iota(I32, (1, QUAD * width), 1)
    target = jnp.full((1, QUAD * width), -1, I32)
    for i in range(QUAD):
        k = lane - i * width
        here = (k >= 0) & (k < rank[i])
        target = jnp.where(here, first[i] + k, target)
    row = lax.broadcasted_iota(I32, (rows, QUAD * width), 0)
    return jnp.where(row == target, 1.0, 0.0).astype(BF16)


def order_of(plan, g, index):
    first, _, _ = spots(plan, g)
    seg = jnp.zeros(index.shape, I32)
    for i in range(1, QUAD):
        seg = seg + jnp.where(index >= first[i], 1, 0)
    return seg


def mixing(rows, levels, lags, plan, x, v, t, out, a, place, maps, far, far_in, near, near_in, summed, summed_in,
           keep_next, keep_own, state, state_in, done, send, recv, out_sem):
    col, z = lax.axis_index("col"), lax.axis_index("rank")
    width = v.shape[1]
    chunks = out.shape[0]

    def flipped(bit):
        return col + bit - 2 * bit * lax.rem(lax.div(col, bit), 2)

    def at(step):
        return lax.rem(z + step, 4)

    n_col = lax.axis_size("col")
    partners = [(flipped(n_col >> (l + 1)), z) for l in range(levels)]

    barrier = pltpu.get_barrier_semaphore()
    for peer in [(col, at(1)), (col, at(3))] + partners:
        pl.semaphore_signal(barrier, inc=1, device_id=peer, device_id_type=MESH)
    pl.semaphore_wait(barrier, 2 + levels)

    def remote(kind, j, src, dst, peer):
        return pltpu.make_async_remote_copy(
            src_ref=src, dst_ref=dst, send_sem=send.at[kind, j], recv_sem=recv.at[kind, j],
            device_id=peer, device_id_type=MESH)

    FAR, NEAR, SUM, AHEAD, BACK, ON, LEVEL = 0, 1, 2, 3, 4, 5, 6

    def sides(j):
        h = lax.rem(j, 2)
        return at(1 + 2 * h), at(3 - 2 * h), at(2)

    def far_copy(j):
        ahead, _, _ = sides(j)
        return remote(FAR, j, far.at[j], far_in.at[j], (col, ahead))

    def near_copy(j):
        _, back, _ = sides(j)
        return remote(NEAR, j, near.at[j], near_in.at[j], (col, back))

    def sum_copy(j):
        ahead, _, _ = sides(j)
        return remote(SUM, j, summed.at[j], summed_in.at[j], (col, ahead))

    def level_copy(l, j):
        return remote(LEVEL + l, j, state.at[l, j], state_in.at[l, j], partners[l])

    def ahead_copy(j, q):
        ahead, _, _ = sides(j)
        return remote(AHEAD, j, done.at[j, q], done.at[j, q], (col, ahead))

    def back_copy(j, q):
        _, back, _ = sides(j)
        return remote(BACK, j, done.at[j, q], done.at[j, q], (col, back))

    def on_copy(j, q):
        ahead, _, _ = sides(j)
        return remote(ON, j, done.at[j, q], done.at[j, q], (col, ahead))

    def out_copy(j):
        return pltpu.make_async_copy(done.at[j], out.at[j], out_sem.at[j])

    def leaf(j):
        g, h = lax.div(j, 2), lax.rem(j, 2)
        ahead, back, across = sides(j)

        @pl.when(h == 0)
        def _():
            p = placing(plan, g, rows, width)
            place[...] = p
            degree = (col * 4 + z) * 128 + lax.broadcasted_iota(I32, (1, 128), 1)
            for i in range(QUAD):
                o = plan[0, QUAD * g + i]
                picked = dot(p[:, i * width:(i + 1) * width], v[o])
                kept = jnp.where(degree >= plan[3, QUAD * g + i], picked, 0.0)
                a[:, i * 128:(i + 1) * 128] = kept.astype(BF16)

        def fields(q):
            parts = []
            for b in range(2):
                batch = 4 * q + 2 * h + b
                parts.append(jnp.concatenate([x[batch, plan[0, QUAD * g + i]] for i in range(QUAD)], axis=1))
            return jnp.concatenate(parts, axis=0)

        sent = dot(a[...], jnp.concatenate([fields(across), fields(back)], axis=0), ((1,), (1,)))
        far[j] = sent[:, :128].astype(BF16)
        near[j] = sent[:, 128:].astype(BF16)
        far_copy(j).start()
        near_copy(j).start()
        kept = dot(a[...], jnp.concatenate([fields(ahead), fields(z)], axis=0), ((1,), (1,)))
        keep_next[j] = kept[:, :128]
        keep_own[j] = kept[:, 128:]

        @pl.when(h == 1)
        def _():
            _, _, filled = spots(plan, g)
            first, _, _ = spots(plan, g)
            lane = lax.broadcasted_iota(I32, (1, rows), 1)
            seg = order_of(plan, g, lane)
            k = lane
            for i in range(1, QUAD):
                k = jnp.where(seg == i, lane - first[i], k)
            k = jnp.where(lane < filled, k, -1000)
            j_row = lax.broadcasted_iota(I32, (2 * width, rows), 0)
            pick_own = jnp.where(j_row == k, 1.0, 0.0).astype(BF16)
            pick_partner = jnp.where(j_row - width == k, 1.0, 0.0).astype(BF16)
            row = lax.broadcasted_iota(I32, (rows, rows), 0)
            same = jnp.where(order_of(plan, g, row) == seg, 1.0, 0.0)
            p = place[...]
            for l in range(levels):
                stack = jnp.concatenate([t[l, plan[0, QUAD * g + i], 0] for i in range(QUAD)], axis=0)
                packed = dot(p, stack).astype(BF16)
                maps[l, g, 0] = (dot(packed, pick_own) * same).astype(BF16)
                maps[l, g, 1] = (dot(packed, pick_partner) * same).astype(BF16)

    def pass_on(j):
        far_copy(j).wait_recv()
        summed[j] = (keep_next[j] + far_in[j].astype(F32)).astype(BF16)
        sum_copy(j).start()

    def first_state(j):
        near_copy(j).wait_recv()
        sum_copy(j).wait_recv()
        total = keep_own[j] + near_in[j].astype(F32) + summed_in[j].astype(F32)
        state[0, j] = total.astype(BF16)
        level_copy(0, j).start()

    def mix(l, j):
        g = lax.div(j, 2)
        level_copy(l, j).wait_recv()
        new = dot(maps[l, g, 0], state[l, j]) + dot(maps[l, g, 1], state_in[l, j])
        return new.astype(BF16)

    def level(l, j):
        state[l + 1, j] = mix(l, j)
        level_copy(l + 1, j).start()

    def last_level(j):
        done[j, z] = mix(levels - 1, j)
        ahead_copy(j, z).start()
        back_copy(j, z).start()

    def hand_on(j):
        _, back, _ = sides(j)
        ahead_copy(j, back).wait_recv()
        on_copy(j, back).start()

    def finish(j):
        ahead, _, across = sides(j)
        back_copy(j, ahead).wait_recv()
        on_copy(j, across).wait_recv()
        out_copy(j).start()

    stages = [leaf, pass_on, first_state]
    stages += [functools.partial(level, l) for l in range(levels - 1)]
    stages += [last_level, hand_on, finish]

    def step(s, carry):
        for lag, stage in zip(lags, stages, strict=True):
            j = s - lag

            @pl.when((j >= 0) & (j < chunks))
            def _(stage=stage, j=j):
                stage(j)

        return carry

    lax.fori_loop(0, chunks + max(lags), step, 0)

    def settle(j, carry):
        _, back, _ = sides(j)
        far_copy(j).wait_send()
        near_copy(j).wait_send()
        sum_copy(j).wait_send()
        for l in range(levels):
            level_copy(l, j).wait_send()
        ahead_copy(j, z).wait_send()
        back_copy(j, z).wait_send()
        on_copy(j, back).wait_send()
        out_copy(j).wait()
        return carry

    lax.fori_loop(0, chunks, settle, 0)


def mixed(rows, cid, plan, x, v, t):
    levels, groups = t.shape[0], x.shape[1] // QUAD
    chunks = 2 * groups
    chunk = (chunks, rows, 128)
    kinds = 6 + levels
    vmem, smem, anywhere = (pl.BlockSpec(memory_space=m) for m in (pltpu.VMEM, pltpu.SMEM, pl.ANY))
    return pl.pallas_call(
        functools.partial(mixing, rows, levels, LAGS),
        out_shape=jax.ShapeDtypeStruct((chunks, 4, rows, 128), BF16),
        in_specs=[smem, vmem, vmem, vmem],
        out_specs=anywhere,
        scratch_shapes=[
            pltpu.VMEM((rows, QUAD * 128), BF16),
            pltpu.VMEM((rows, QUAD * v.shape[1]), BF16),
            pltpu.VMEM((levels, groups, 2, rows, rows), BF16),
            pltpu.VMEM(chunk, BF16), pltpu.VMEM(chunk, BF16),
            pltpu.VMEM(chunk, BF16), pltpu.VMEM(chunk, BF16),
            pltpu.VMEM(chunk, BF16), pltpu.VMEM(chunk, BF16),
            pltpu.VMEM(chunk, F32), pltpu.VMEM(chunk, F32),
            pltpu.VMEM((levels, *chunk), BF16), pltpu.VMEM((levels, *chunk), BF16),
            pltpu.VMEM((chunks, 4, rows, 128), BF16),
            pltpu.SemaphoreType.DMA((kinds, chunks)),
            pltpu.SemaphoreType.DMA((kinds, chunks)),
            pltpu.SemaphoreType.DMA((chunks,)),
        ],
        compiler_params=pltpu.CompilerParams(
            collective_id=cid, has_side_effects=True, vmem_limit_bytes=58 * 2**20),
        cost_estimate=pl.CostEstimate(flops=10**9, bytes_accessed=16 * 2**20, transcendentals=0),
    )(plan, x, v, t)


def writing(rows, plan, s, u, out, buf, sem):
    g, groups = pl.program_id(0), pl.num_programs(0)
    slot = lax.rem(g, 2)
    width = u.shape[1]

    def copies(group, slot):
        return [pltpu.make_async_copy(buf.at[slot, i], out.at[:, plan[0, QUAD * group + i]], sem.at[slot, i])
                for i in range(QUAD)]

    p = placing(plan, g, rows, width)
    packed = [dot(p[:, i * width:(i + 1) * width], u[plan[0, QUAD * g + i]]).astype(BF16) for i in range(QUAD)]
    packed = jnp.concatenate(packed, axis=1)

    @pl.when(g >= 2)
    def _():
        for c in copies(g - 2, slot):
            c.wait()

    for h in range(2):
        for q in range(4):
            points = dot(s[h, q], packed, ((0,), (0,))).astype(BF16)
            for i in range(QUAD):
                for b in range(2):
                    buf[slot, i, 4 * q + 2 * h + b] = points[b * 64:(b + 1) * 64, i * 128:(i + 1) * 128]
    for c in copies(g, slot):
        c.start()

    @pl.when(g == groups - 1)
    def _():
        for c in copies(g - 1, 1 - slot) + copies(g, slot):
            c.wait()


def written(rows, plan, s, u, shape):
    groups = shape[1] // QUAD
    return pl.pallas_call(
        functools.partial(writing, rows),
        out_shape=jax.ShapeDtypeStruct(shape, BF16),
        grid_spec=pltpu.PrefetchScalarGridSpec(
            num_scalar_prefetch=1,
            grid=(groups,),
            in_specs=[pl.BlockSpec((2, 4, rows, 128), lambda g, plan: (g, 0, 0, 0)),
                      pl.BlockSpec(memory_space=pltpu.VMEM)],
            out_specs=pl.BlockSpec(memory_space=pl.ANY),
            scratch_shapes=[pltpu.VMEM((2, QUAD, shape[0], shape[2], shape[3]), BF16),
                            pltpu.SemaphoreType.DMA((2, QUAD))],
        ),
        compiler_params=pltpu.CompilerParams(vmem_limit_bytes=48 * 2**20),
    )(plan, s, u)


def turned(row):
    n = row.shape[1]
    i, j = (lax.broadcasted_iota(I32, (n, n), d) for d in (0, 1))
    return jnp.sum(jnp.where(i == j, jnp.broadcast_to(row, (n, n)), 0.0), axis=1, keepdims=True)


def planning(heights, orders, ranks, plan, pick):
    n = ranks.shape[0]
    groups = n // QUAD
    i, j = (lax.broadcasted_iota(I32, (n, n), d).astype(F32) for d in (0, 1))
    lane = lax.broadcasted_iota(I32, (1, n), 1).astype(F32)
    rank = ranks[...].reshape(1, n).astype(F32)
    order = orders[...].reshape(1, n).astype(F32)
    rank_down, order_down = turned(rank), turned(order)
    ahead = (rank_down > rank) | ((rank_down == rank) & (i < j))
    spot = jnp.sum(jnp.where(ahead, 1.0, 0.0), axis=0, keepdims=True)
    turn = sum(jnp.where(spot >= groups * m, 1.0, 0.0) for m in range(1, QUAD))
    k = spot - groups * turn
    back = (turn == 1.0) | (turn == 3.0)
    slot = QUAD * jnp.where(back, groups - 1.0 - k, k) + turn
    here = turned(slot) == j

    def dealt(values):
        return jnp.sum(jnp.where(here, values, 0.0), axis=0, keepdims=True)

    rank_here = dealt(rank_down)
    group = sum(jnp.where(lane >= QUAD * m, 1.0, 0.0) for m in range(1, groups))
    earlier = (turned(group) == group) & (i < j)
    first = jnp.sum(jnp.where(earlier, turned(rank_here), 0.0), axis=0, keepdims=True)
    for at, row in enumerate((dealt(i), first, rank_here, dealt(order_down))):
        plan[at:at + 1, :] = row.astype(I32)
    most = jnp.max(first + rank_here)
    pick[0] = sum((most > height).astype(I32) for height in heights[:-1])


def planned(heights, orders, ranks):
    vmem, smem = (pl.BlockSpec(memory_space=m) for m in (pltpu.VMEM, pltpu.SMEM))
    return pl.pallas_call(
        functools.partial(planning, heights),
        out_shape=(jax.ShapeDtypeStruct((4, ranks.shape[0]), I32), jax.ShapeDtypeStruct((1,), I32)),
        in_specs=[vmem, vmem],
        out_specs=(vmem, smem),
    )(orders, ranks)


def shards(coefficients, v_factors, transfer, u_factors, orders, ranks):
    most = QUAD * v_factors.shape[1]
    heights = tuple(most * part // 16 for part in PARTS)
    plan, pick = planned(heights, orders, ranks)

    def branch(rows, cid, plan, x, v, t, u):
        return written(rows, plan, mixed(rows, cid, plan, x, v, t), u, x.shape)

    branches = [functools.partial(branch, rows, 1 + at) for at, rows in enumerate(heights)]
    return lax.switch(pick[0], branches, plan, coefficients, v_factors, transfer, u_factors)


def solution(mesh):
    placed = (
        P(None, None, None, ("col", "rank")),
        P(None, None, ("col", "rank")),
        P(None, None, "col", None, None),
        P(None, None, ("col", "rank")),
        P(),
        P(),
    )
    return jax.shard_map(
        shards,
        mesh=mesh,
        in_specs=placed,
        out_specs=P(None, None, None, ("col", "rank")),
        check_vma=False,
    )
```

```python
import functools
import math

import jax
import jax.numpy as jnp
from jax import lax
from jax.experimental import pallas as pl
from jax.experimental.pallas import tpu as pltpu
from jax.sharding import PartitionSpec as P

MESH = pl.DeviceIdType.MESH
BF16, F32, I32 = jnp.bfloat16, jnp.float32, jnp.int32
QUAD = 4
LAGS = (0, 4, 7, 8, 10, 13, 16, 20, 23)
PARTS = (10, 11, 12, 16)


def dot(a, b, dims=((1,), (0,))):
    return lax.dot_general(a, b, (dims, ((), ())), preferred_element_type=F32)


def spots(plan, g):
    first = [plan[1, QUAD * g + i] for i in range(QUAD)]
    rank = [plan[2, QUAD * g + i] for i in range(QUAD)]
    return first, rank, first[QUAD - 1] + rank[QUAD - 1]


def placing(plan, g, rows, width):
    first, rank, _ = spots(plan, g)
    lane = lax.broadcasted_iota(I32, (1, QUAD * width), 1)
    target = jnp.full((1, QUAD * width), -1, I32)
    for i in range(QUAD):
        k = lane - i * width
        here = (k >= 0) & (k < rank[i])
        target = jnp.where(here, first[i] + k, target)
    row = lax.broadcasted_iota(I32, (rows, QUAD * width), 0)
    return jnp.where(row == target, 1.0, 0.0).astype(BF16)


def order_of(plan, g, index):
    first, _, _ = spots(plan, g)
    seg = jnp.zeros(index.shape, I32)
    for i in range(1, QUAD):
        seg = seg + jnp.where(index >= first[i], 1, 0)
    return seg


def mixing(rows, lags, plan, x_hbm, v_hbm, t_hbm, u_hbm, out, x_first, x_second, v, t, u, a, u_packed, maps, far, far_in, near, near_in,
           summed, summed_in, keep_next, keep_own, blocks, mid, mid_in, done, t_in, send, recv, t_send, t_recv, load_sem):
    col, z = lax.axis_index("col"), lax.axis_index("rank")
    n_col = lax.axis_size("col")
    stride = n_col // 4
    me = lax.div(col, stride)
    half = stride // 2
    width = v.shape[1]
    chunks = done.shape[0]

    def at(step):
        return lax.rem(z + step, 4)

    def ring(step):
        return lax.rem(me + step, 4)

    def block(place):
        return place * stride + lax.rem(col, stride)

    pair = me + 1 - 2 * lax.rem(me, 2)
    opposite = ring(2)
    pair_opposite = lax.rem(pair + 2, 4)
    last = col + half - 2 * half * lax.rem(lax.div(col, half), 2)

    loads = [pltpu.make_async_copy(src, dst, load_sem.at[i]) for i, (src, dst) in enumerate(
        [(v_hbm, v), (x_hbm.at[:, 0], x_first), (x_hbm.at[:, 1], x_second), (t_hbm, t), (u_hbm, u)])]
    for load in loads:
        load.start()

    peers = [(col, at(1)), (col, at(3)), (block(ring(1)), z), (block(ring(3)), z), (last, z)]
    barrier = pltpu.get_barrier_semaphore()
    for peer in peers:
        pl.semaphore_signal(barrier, inc=1, device_id=peer, device_id_type=MESH)
    pl.semaphore_wait(barrier, len(peers))

    t_copy = pltpu.make_async_remote_copy(
        src_ref=t_hbm.at[0], dst_ref=t_in, send_sem=t_send, recv_sem=t_recv,
        device_id=(block(pair), z), device_id_type=MESH)
    t_copy.start()

    def remote(kind, j, src, dst, peer):
        return pltpu.make_async_remote_copy(
            src_ref=src, dst_ref=dst, send_sem=send.at[kind, j], recv_sem=recv.at[kind, j],
            device_id=peer, device_id_type=MESH)

    def sides(j):
        h = lax.rem(j, 2)
        return at(1 + 2 * h), at(3 - 2 * h), at(2)

    def ring_sides(j):
        h = lax.rem(j, 2)
        return ring(1 + 2 * h), ring(3 - 2 * h)

    def far_copy(j):
        ahead, _, _ = sides(j)
        return remote(0, j, far.at[j], far_in.at[j], (col, ahead))

    def near_copy(j):
        _, back, _ = sides(j)
        return remote(1, j, near.at[j], near_in.at[j], (col, back))

    def sum_copy(j):
        ahead, _, _ = sides(j)
        return remote(2, j, summed.at[j], summed_in.at[j], (col, ahead))

    def ahead_copy(j, q):
        ahead, _, _ = sides(j)
        return remote(3, j, done.at[j, q], done.at[j, q], (col, ahead))

    def back_copy(j, q):
        _, back, _ = sides(j)
        return remote(4, j, done.at[j, q], done.at[j, q], (col, back))

    def on_copy(j, q):
        ahead, _, _ = sides(j)
        return remote(5, j, done.at[j, q], done.at[j, q], (col, ahead))

    def ring_ahead(j, c):
        ahead, _ = ring_sides(j)
        return remote(6, j, blocks.at[j, c], blocks.at[j, c], (block(ahead), z))

    def ring_back(j, c):
        _, back = ring_sides(j)
        return remote(7, j, blocks.at[j, c], blocks.at[j, c], (block(back), z))

    def ring_on(j, c):
        ahead, _ = ring_sides(j)
        return remote(8, j, blocks.at[j, c], blocks.at[j, c], (block(ahead), z))

    def mid_copy(j):
        return remote(9, j, mid.at[j], mid_in.at[j], (last, z))

    def leaf(j):
        g, h = lax.div(j, 2), lax.rem(j, 2)
        ahead, back, across = sides(j)

        def halved(x):
            def fields(q):
                return jnp.concatenate([
                    jnp.concatenate([x[q, b, plan[0, QUAD * g + i]] for i in range(QUAD)], axis=1)
                    for b in range(2)], axis=0)

            sent = dot(a[...], jnp.concatenate([fields(across), fields(back)], axis=0), ((1,), (1,)))
            far[j] = sent[:, :128].astype(BF16)
            near[j] = sent[:, 128:].astype(BF16)
            far_copy(j).start()
            near_copy(j).start()
            kept = dot(a[...], jnp.concatenate([fields(ahead), fields(z)], axis=0), ((1,), (1,)))
            keep_next[j] = kept[:, :128]
            keep_own[j] = kept[:, 128:]

        @pl.when(j == 0)
        def _():
            loads[0].wait()

        @pl.when(h == 0)
        def _():
            first, _, _ = spots(plan, g)
            packed = dot(placing(plan, g, rows, width),
                         jnp.concatenate([v[plan[0, QUAD * g + i]] for i in range(QUAD)], axis=0))
            seg = order_of(plan, g, lax.broadcasted_iota(I32, (rows, 1), 0))
            degree = (col * 4 + z) * 128 + lax.broadcasted_iota(I32, (1, 128), 1)
            for i in range(QUAD):
                kept = (seg == i) & (degree >= plan[3, QUAD * g + i])
                a[:, i * 128:(i + 1) * 128] = jnp.where(kept, packed, 0.0).astype(BF16)

        @pl.when(j == 0)
        def _():
            loads[1].wait()

        @pl.when(j == 1)
        def _():
            loads[2].wait()

        @pl.when(h == 0)
        def _():
            halved(x_first)

        @pl.when(h == 1)
        def _():
            halved(x_second)

    def prepare(j):
        g = lax.div(j, 2)

        @pl.when(j == 1)
        def _():
            loads[3].wait()
            loads[4].wait()
            t_copy.wait_recv()

        first, _, filled = spots(plan, g)
        lane = lax.broadcasted_iota(I32, (1, rows), 1)
        seg = order_of(plan, g, lane)
        k = lane
        for i in range(1, QUAD):
            k = jnp.where(seg == i, lane - first[i], k)
        k = jnp.where(lane < filled, k, -1000)
        j_row = lax.broadcasted_iota(I32, (2 * width, rows), 0)
        pick_own = jnp.where(j_row == k, 1.0, 0.0).astype(BF16)
        pick_partner = jnp.where(j_row - width == k, 1.0, 0.0).astype(BF16)
        row = lax.broadcasted_iota(I32, (rows, 1), 0)
        same = order_of(plan, g, row) == seg
        p = placing(plan, g, rows, width)
        u_packed[g] = dot(p, jnp.concatenate([u[plan[0, QUAD * g + i]] for i in range(QUAD)], axis=0)).astype(BF16)
        reads = [lambda o: t[0, o, 0], lambda o: t_in[o, 0], lambda o: t[1, o, 0], lambda o: t[2, o, 0]]
        for m in range(0, 4, 2):
            stack = jnp.concatenate([
                jnp.concatenate([read(plan[0, QUAD * g + i]) for read in reads[m:m + 2]], axis=1)
                for i in range(QUAD)], axis=0)
            packed = dot(p, stack).astype(BF16)
            for n in range(2):
                part = packed[:, n * 2 * width:(n + 1) * 2 * width]
                maps[m + n, g, 0] = jnp.where(same, dot(part, pick_own), 0.0).astype(BF16)
                maps[m + n, g, 1] = jnp.where(same, dot(part, pick_partner), 0.0).astype(BF16)

    def pass_on(j):
        far_copy(j).wait_recv()
        summed[j] = (keep_next[j] + far_in[j].astype(F32)).astype(BF16)
        sum_copy(j).start()

    def first_state(j):
        near_copy(j).wait_recv()
        sum_copy(j).wait_recv()
        total = keep_own[j] + near_in[j].astype(F32) + summed_in[j].astype(F32)
        blocks[j, me] = total.astype(BF16)
        ring_ahead(j, me).start()
        ring_back(j, me).start()

    def ring_hand_on(j):
        _, back = ring_sides(j)
        ring_ahead(j, back).wait_recv()
        ring_on(j, back).start()

    def mix(m, g, own, partner):
        return (dot(maps[m, g, 0], own) + dot(maps[m, g, 1], partner)).astype(BF16)

    def two_levels(j):
        g = lax.div(j, 2)
        for c in (j - 1, j):
            ahead, _ = ring_sides(c)
            ring_back(c, ahead).wait_recv()
            ring_on(c, opposite).wait_recv()

        def both(c):
            return jnp.concatenate([blocks[j - 1, c], blocks[j, c]], axis=1)

        own = mix(0, g, both(me), both(opposite))
        partner = mix(1, g, both(pair), both(pair_opposite))
        new = mix(2, g, own, partner)
        mid[g, 0] = new[:, :128]
        mid[g, 1] = new[:, 128:]
        mid_copy(g).start()

    def last_level(j):
        g = lax.div(j, 2)
        mid_copy(g).wait_recv()
        new = mix(3, g, jnp.concatenate([mid[g, 0], mid[g, 1]], axis=1),
                  jnp.concatenate([mid_in[g, 0], mid_in[g, 1]], axis=1))
        for n, c in enumerate((j - 1, j)):
            done[c, z] = new[:, n * 128:(n + 1) * 128]
            ahead_copy(c, z).start()
            back_copy(c, z).start()

    def hand_on(j):
        _, back, _ = sides(j)
        ahead_copy(j, back).wait_recv()
        on_copy(j, back).start()

    def finish(j):
        ahead, _, across = sides(j)
        back_copy(j, ahead).wait_recv()
        on_copy(j, across).wait_recv()
        g, h = lax.div(j, 2), lax.rem(j, 2)
        seg = order_of(plan, g, lax.broadcasted_iota(I32, (rows, 1), 0))
        factors = u_packed[g]
        factors = jnp.concatenate([jnp.where(seg == i, factors, jnp.zeros_like(factors)) for i in range(QUAD)], axis=1)
        points = dot(jnp.concatenate([done[j, q] for q in range(4)], axis=1), factors, ((0,), (0,))).astype(BF16)
        for q in range(4):
            for b in range(2):
                row = (2 * q + b) * 64
                for i in range(QUAD):
                    out[g, i, 4 * q + 2 * h + b] = points[row:row + 64, i * 128:(i + 1) * 128]

    paired = (prepare, two_levels, last_level)
    stages = (leaf, pass_on, first_state, prepare, ring_hand_on, two_levels, last_level, hand_on, finish)

    def step(s, carry):
        for at in (7, 6, 5, 4, 2, 1, 0, 3, 8):
            lag, stage = lags[at], stages[at]
            j = s - lag
            due = (j >= 0) & (j < chunks)
            if stage in paired:
                due = due & (lax.rem(j, 2) == 1)

            @pl.when(due)
            def _(stage=stage, j=j):
                stage(j)

        return carry

    lax.fori_loop(0, chunks + max(lags), step, 0)

    def settle(j, carry):
        _, back, _ = sides(j)
        _, ring_from = ring_sides(j)
        sent = [far_copy(j), near_copy(j), sum_copy(j), ahead_copy(j, z), back_copy(j, z), on_copy(j, back),
                ring_ahead(j, me), ring_back(j, me), ring_on(j, ring_from)]
        for copy in sent:
            copy.wait_send()

        @pl.when(lax.rem(j, 2) == 1)
        def _():
            mid_copy(lax.div(j, 2)).wait_send()

        return carry

    t_copy.wait_send()
    lax.fori_loop(0, chunks, settle, 0)


def mixed(rows, cid, plan, x, v, t, u):
    batches, orders, fields, points = x.shape
    groups = orders // QUAD
    chunks = 2 * groups
    chunk = (chunks, rows, 128)
    smem, vmem, hbm = (pl.BlockSpec(memory_space=m) for m in (pltpu.SMEM, pltpu.VMEM, pltpu.HBM))
    x = x.reshape(4, 2, batches // 8, orders, fields, points)
    arrays = [
        *[((4, *x.shape[2:]), BF16)] * 2, (v.shape, BF16), (t.shape, BF16), (u.shape, BF16),
        ((rows, QUAD * 128), BF16), ((groups, rows, 128), BF16), ((4, groups, 2, rows, rows), BF16),
        *[(chunk, BF16)] * 6, *[(chunk, F32)] * 2,
        ((chunks, 4, rows, 128), BF16), *[((groups, 2, rows, 128), BF16)] * 2, ((chunks, 4, rows, 128), BF16),
        (t.shape[1:], BF16)]
    size = sum(math.prod(shape[:-1]) * -(-shape[-1] // 128) * 128 * jnp.dtype(kind).itemsize for shape, kind in arrays)
    return pl.pallas_call(
        functools.partial(mixing, rows, LAGS),
        out_shape=jax.ShapeDtypeStruct((groups, QUAD, batches, fields, points), BF16),
        in_specs=[smem, hbm, hbm, hbm, hbm],
        out_specs=vmem,
        scratch_shapes=[
            *[pltpu.VMEM(shape, kind) for shape, kind in arrays],
            pltpu.SemaphoreType.DMA((10, chunks)),
            pltpu.SemaphoreType.DMA((10, chunks)),
            pltpu.SemaphoreType.DMA,
            pltpu.SemaphoreType.DMA,
            pltpu.SemaphoreType.DMA((5,)),
        ],
        compiler_params=pltpu.CompilerParams(
            collective_id=cid, has_side_effects=True, vmem_limit_bytes=size + 13 * 2**20),
        cost_estimate=pl.CostEstimate(flops=10**9, bytes_accessed=16 * 2**20, transcendentals=0),
    )(plan, x, v, t, u)


def dealing(plan, packed, out, sem):
    groups = packed.shape[0]
    copies = [pltpu.make_async_copy(packed.at[g, i], out.at[:, plan[0, QUAD * g + i]], sem.at[g, i])
              for g in range(groups) for i in range(QUAD)]
    for copy in copies:
        copy.start()
    for copy in copies:
        copy.wait()


def dealt_out(plan, packed, shape):
    smem, vmem, hbm = (pl.BlockSpec(memory_space=m) for m in (pltpu.SMEM, pltpu.VMEM, pltpu.HBM))
    return pl.pallas_call(
        dealing,
        out_shape=jax.ShapeDtypeStruct(shape, BF16),
        in_specs=[smem, vmem],
        out_specs=hbm,
        scratch_shapes=[pltpu.SemaphoreType.DMA(packed.shape[:2])],
        compiler_params=pltpu.CompilerParams(vmem_limit_bytes=16 * 2**20),
    )(plan, packed)


def settled(result):
    anywhere = pl.BlockSpec(memory_space=pl.ANY)
    return pl.pallas_call(
        lambda given, out: None,
        out_shape=jax.ShapeDtypeStruct(result.shape, result.dtype),
        in_specs=[anywhere],
        out_specs=anywhere,
        input_output_aliases={0: 0},
    )(result)


def turned(row):
    n = row.shape[1]
    i, j = (lax.broadcasted_iota(I32, (n, n), d) for d in (0, 1))
    return jnp.sum(jnp.where(i == j, jnp.broadcast_to(row, (n, n)), 0.0), axis=1, keepdims=True)


def planning(heights, orders, ranks, plan, pick):
    n = ranks.shape[0]
    groups = n // QUAD
    i, j = (lax.broadcasted_iota(I32, (n, n), d).astype(F32) for d in (0, 1))
    lane = lax.broadcasted_iota(I32, (1, n), 1).astype(F32)
    rank = ranks[...].reshape(1, n).astype(F32)
    order = orders[...].reshape(1, n).astype(F32)
    rank_down, order_down = turned(rank), turned(order)
    ahead = (rank_down > rank) | ((rank_down == rank) & (i < j))
    spot = jnp.sum(jnp.where(ahead, 1.0, 0.0), axis=0, keepdims=True)
    turn = sum(jnp.where(spot >= groups * m, 1.0, 0.0) for m in range(1, QUAD))
    k = spot - groups * turn
    back = (turn == 1.0) | (turn == 3.0)
    slot = QUAD * jnp.where(back, groups - 1.0 - k, k) + turn
    here = turned(slot) == j

    def dealt(values):
        return jnp.sum(jnp.where(here, values, 0.0), axis=0, keepdims=True)

    rank_here = dealt(rank_down)
    group = sum(jnp.where(lane >= QUAD * m, 1.0, 0.0) for m in range(1, groups))
    earlier = (turned(group) == group) & (i < j)
    first = jnp.sum(jnp.where(earlier, turned(rank_here), 0.0), axis=0, keepdims=True)
    for at, row in enumerate((dealt(i), first, rank_here, dealt(order_down))):
        plan[at:at + 1, :] = row.astype(I32)
    most = jnp.max(first + rank_here)
    pick[0] = sum((most > height).astype(I32) for height in heights[:-1])


def planned(heights, orders, ranks):
    vmem, smem = (pl.BlockSpec(memory_space=m) for m in (pltpu.VMEM, pltpu.SMEM))
    return pl.pallas_call(
        functools.partial(planning, heights),
        out_shape=(jax.ShapeDtypeStruct((4, ranks.shape[0]), I32), jax.ShapeDtypeStruct((1,), I32)),
        in_specs=[vmem, vmem],
        out_specs=(vmem, smem),
    )(orders, ranks)


def shards(coefficients, v_factors, transfer, u_factors, orders, ranks):
    most = QUAD * v_factors.shape[1]
    heights = tuple(most * part // 16 for part in PARTS)
    plan, pick = planned(heights, orders, ranks)

    def branch(rows, cid, plan, x, v, t, u):
        return dealt_out(plan, mixed(rows, cid, plan, x, v, t, u), x.shape)

    branches = [functools.partial(branch, rows, 1 + at) for at, rows in enumerate(heights)]
    return settled(lax.switch(pick[0], branches, plan, coefficients, v_factors, transfer, u_factors))


def solution(mesh):
    placed = (
        P(None, None, None, ("col", "rank")),
        P(None, None, ("col", "rank")),
        P(None, None, "col", None, None),
        P(None, None, ("col", "rank")),
        P(),
        P(),
    )
    return jax.shard_map(
        shards,
        mesh=mesh,
        in_specs=placed,
        out_specs=P(None, None, None, ("col", "rank")),
        check_vma=False,
    )
```

```python
import functools
import math

import jax
import jax.numpy as jnp
from jax import lax
from jax.experimental import pallas as pl
from jax.experimental.pallas import tpu as pltpu
from jax.sharding import PartitionSpec as P

MESH = pl.DeviceIdType.MESH
BF16, F32, I32 = jnp.bfloat16, jnp.float32, jnp.int32
QUAD = 4
LAGS = (0, 4, 8, 13, 11, 14, 18, 22, 26, 27)
ORDER = (0, 7, 6, 5, 4, 2, 1, 3, 8, 9)
PARTS = (10, 11, 12, 16)


def dot(a, b, dims=((1,), (0,))):
    return lax.dot_general(a, b, (dims, ((), ())), preferred_element_type=F32)


def spots(plan, g):
    first = [plan[1, QUAD * g + i] for i in range(QUAD)]
    rank = [plan[2, QUAD * g + i] for i in range(QUAD)]
    return first, rank, first[QUAD - 1] + rank[QUAD - 1]


def placing(plan, g, rows, width):
    first, rank, _ = spots(plan, g)
    lane = lax.broadcasted_iota(I32, (1, QUAD * width), 1)
    target = jnp.full((1, QUAD * width), -1, I32)
    for i in range(QUAD):
        k = lane - i * width
        here = (k >= 0) & (k < rank[i])
        target = jnp.where(here, first[i] + k, target)
    row = lax.broadcasted_iota(I32, (rows, QUAD * width), 0)
    return jnp.where(row == target, 1.0, 0.0).astype(BF16)


def order_of(plan, g, index):
    first, _, _ = spots(plan, g)
    seg = jnp.zeros(index.shape, I32)
    for i in range(1, QUAD):
        seg = seg + jnp.where(index >= first[i], 1, 0)
    return seg


def mixing(rows, lags, plan, x_hbm, v_hbm, t_hbm, u_hbm, out, *scratch):
    *x, v, t, u, a, u_packed, maps, far, far_in, near, near_in, summed, summed_in, keep_next, keep_own, blocks, mid, mid_in, \
        done, t_in, send, recv, t_send, t_recv, load_sem = scratch
    col, z = lax.axis_index("col"), lax.axis_index("rank")
    n_col = lax.axis_size("col")
    stride = n_col // 4
    me = lax.div(col, stride)
    half = stride // 2
    width = v.shape[1]
    chunks = done.shape[0]

    def at(step):
        return lax.rem(z + step, 4)

    def ring(step):
        return lax.rem(me + step, 4)

    def block(place):
        return place * stride + lax.rem(col, stride)

    pair = me + 1 - 2 * lax.rem(me, 2)
    opposite = ring(2)
    pair_opposite = lax.rem(pair + 2, 4)
    last = col + half - 2 * half * lax.rem(lax.div(col, half), 2)

    quarters = [(at(2), at(3 - 2 * h), at(1 + 2 * h), z) for h in range(2)]
    x_loads = [(x_hbm.at[q, h], x[4 * h + i]) for h in range(2) for i, q in enumerate(quarters[h])]
    loads = [pltpu.make_async_copy(src, dst, load_sem.at[i])
             for i, (src, dst) in enumerate([(v_hbm, v), *x_loads, (t_hbm, t), (u_hbm, u)])]
    for load in loads:
        load.start()

    peers = [(col, at(1)), (col, at(3)), (block(ring(1)), z), (block(ring(3)), z), (last, z)]
    barrier = pltpu.get_barrier_semaphore()
    for peer in peers:
        pl.semaphore_signal(barrier, inc=1, device_id=peer, device_id_type=MESH)
    pl.semaphore_wait(barrier, len(peers))

    t_copy = pltpu.make_async_remote_copy(
        src_ref=t_hbm.at[0], dst_ref=t_in, send_sem=t_send, recv_sem=t_recv,
        device_id=(block(pair), z), device_id_type=MESH)
    t_copy.start()

    def remote(kind, j, src, dst, peer):
        return pltpu.make_async_remote_copy(
            src_ref=src, dst_ref=dst, send_sem=send.at[kind, j], recv_sem=recv.at[kind, j],
            device_id=peer, device_id_type=MESH)

    def sides(j):
        h = lax.rem(j, 2)
        return at(1 + 2 * h), at(3 - 2 * h), at(2)

    def ring_sides(j):
        h = lax.rem(j, 2)
        return ring(1 + 2 * h), ring(3 - 2 * h)

    def far_copy(j):
        ahead, _, _ = sides(j)
        return remote(0, j, far.at[j], far_in.at[j], (col, ahead))

    def near_copy(j):
        _, back, _ = sides(j)
        return remote(1, j, near.at[j], near_in.at[j], (col, back))

    def sum_copy(j):
        ahead, _, _ = sides(j)
        return remote(2, j, summed.at[j], summed_in.at[j], (col, ahead))

    def ahead_copy(j, q):
        ahead, _, _ = sides(j)
        return remote(3, j, done.at[j, q], done.at[j, q], (col, ahead))

    def back_copy(j, q):
        _, back, _ = sides(j)
        return remote(4, j, done.at[j, q], done.at[j, q], (col, back))

    def on_copy(j, q):
        ahead, _, _ = sides(j)
        return remote(5, j, done.at[j, q], done.at[j, q], (col, ahead))

    def ring_ahead(j, c):
        ahead, _ = ring_sides(j)
        return remote(6, j, blocks.at[j, c], blocks.at[j, c], (block(ahead), z))

    def ring_back(j, c):
        _, back = ring_sides(j)
        return remote(7, j, blocks.at[j, c], blocks.at[j, c], (block(back), z))

    def ring_on(j, c):
        ahead, _ = ring_sides(j)
        return remote(8, j, blocks.at[j, c], blocks.at[j, c], (block(ahead), z))

    def mid_copy(j):
        return remote(9, j, mid.at[j], mid_in.at[j], (last, z))

    def leaf(j):
        g, h = lax.div(j, 2), lax.rem(j, 2)

        def halved(half):
            parts = x[4 * half:4 * half + 4]

            def fields(part):
                return jnp.concatenate([
                    jnp.concatenate([part[b, plan[0, QUAD * g + i]] for i in range(QUAD)], axis=1)
                    for b in range(2)], axis=0)

            def leaves(at):
                @pl.when(j == half)
                def _():
                    loads[1 + 4 * half + at].wait()
                    loads[2 + 4 * half + at].wait()

                return dot(a[...], jnp.concatenate([fields(parts[at]), fields(parts[at + 1])], axis=0), ((1,), (1,)))

            sent = leaves(0)
            far[j] = sent[:, :128].astype(BF16)
            near[j] = sent[:, 128:].astype(BF16)
            far_copy(j).start()
            near_copy(j).start()
            kept = leaves(2)
            keep_next[j] = kept[:, :128]
            keep_own[j] = kept[:, 128:]

        @pl.when(j == 0)
        def _():
            loads[0].wait()

        @pl.when(h == 0)
        def _():
            first, _, _ = spots(plan, g)
            packed = dot(placing(plan, g, rows, width),
                         jnp.concatenate([v[plan[0, QUAD * g + i]] for i in range(QUAD)], axis=0))
            seg = order_of(plan, g, lax.broadcasted_iota(I32, (rows, 1), 0))
            degree = (col * 4 + z) * 128 + lax.broadcasted_iota(I32, (1, 128), 1)
            for i in range(QUAD):
                kept = (seg == i) & (degree >= plan[3, QUAD * g + i])
                a[:, i * 128:(i + 1) * 128] = jnp.where(kept, packed, 0.0).astype(BF16)

        @pl.when(h == 0)
        def _():
            halved(0)

        @pl.when(h == 1)
        def _():
            halved(1)

    def prepare(j):
        g = lax.div(j, 2)

        @pl.when(j == 1)
        def _():
            loads[9].wait()
            loads[10].wait()
            t_copy.wait_recv()

        first, _, filled = spots(plan, g)
        lane = lax.broadcasted_iota(I32, (1, rows), 1)
        seg = order_of(plan, g, lane)
        k = lane
        for i in range(1, QUAD):
            k = jnp.where(seg == i, lane - first[i], k)
        k = jnp.where(lane < filled, k, -1000)
        j_row = lax.broadcasted_iota(I32, (2 * width, rows), 0)
        pick_own = jnp.where(j_row == k, 1.0, 0.0).astype(BF16)
        pick_partner = jnp.where(j_row - width == k, 1.0, 0.0).astype(BF16)
        row = lax.broadcasted_iota(I32, (rows, 1), 0)
        same = order_of(plan, g, row) == seg
        p = placing(plan, g, rows, width)
        u_packed[g] = dot(p, jnp.concatenate([u[plan[0, QUAD * g + i]] for i in range(QUAD)], axis=0)).astype(BF16)
        reads = [lambda o: t[0, o, 0], lambda o: t_in[o, 0], lambda o: t[1, o, 0], lambda o: t[2, o, 0]]
        parts = []
        for m in range(0, 4, 2):
            stack = jnp.concatenate([
                jnp.concatenate([read(plan[0, QUAD * g + i]) for read in reads[m:m + 2]], axis=1)
                for i in range(QUAD)], axis=0)
            packed = dot(p, stack).astype(BF16)
            parts += [packed[:, :2 * width], packed[:, 2 * width:]]
        parts = jnp.concatenate(parts, axis=0)
        for side, pick in enumerate((pick_own, pick_partner)):
            placed = dot(parts, pick)
            for m in range(4):
                maps[m, g, side] = jnp.where(same, placed[m * rows:(m + 1) * rows], 0.0).astype(BF16)

    def pass_on(j):
        far_copy(j).wait_recv()
        summed[j] = (keep_next[j] + far_in[j].astype(F32)).astype(BF16)
        sum_copy(j).start()

    def first_state(j):
        near_copy(j).wait_recv()
        sum_copy(j).wait_recv()
        total = keep_own[j] + near_in[j].astype(F32) + summed_in[j].astype(F32)
        blocks[j, me] = total.astype(BF16)
        ring_ahead(j, me).start()
        ring_back(j, me).start()

    def ring_hand_on(j):
        _, back = ring_sides(j)
        ring_ahead(j, back).wait_recv()
        ring_on(j, back).start()

    def mix(m, g, own, partner):
        return (dot(maps[m, g, 0], own) + dot(maps[m, g, 1], partner)).astype(BF16)

    def two_levels(j):
        g = lax.div(j, 2)
        for c in (j - 1, j):
            ahead, _ = ring_sides(c)
            ring_back(c, ahead).wait_recv()
            ring_on(c, opposite).wait_recv()

        def both(c):
            return jnp.concatenate([blocks[j - 1, c], blocks[j, c]], axis=1)

        own = mix(0, g, both(me), both(opposite))
        partner = mix(1, g, both(pair), both(pair_opposite))
        new = mix(2, g, own, partner)
        mid[g, 0] = new[:, :128]
        mid[g, 1] = new[:, 128:]
        mid_copy(g).start()

    def last_level(j):
        g = lax.div(j, 2)
        mid_copy(g).wait_recv()
        new = mix(3, g, jnp.concatenate([mid[g, 0], mid[g, 1]], axis=1),
                  jnp.concatenate([mid_in[g, 0], mid_in[g, 1]], axis=1))
        for n, c in enumerate((j - 1, j)):
            done[c, z] = new[:, n * 128:(n + 1) * 128]
            ahead_copy(c, z).start()
            back_copy(c, z).start()

    def hand_on(j):
        _, back, _ = sides(j)
        ahead_copy(j, back).wait_recv()
        on_copy(j, back).start()

    def finish(j):
        ahead, _, across = sides(j)
        back_copy(j, ahead).wait_recv()
        on_copy(j, across).wait_recv()
        g, h = lax.div(j, 2), lax.rem(j, 2)
        seg = order_of(plan, g, lax.broadcasted_iota(I32, (rows, 1), 0))
        factors = u_packed[g]
        factors = jnp.concatenate([jnp.where(seg == i, factors, jnp.zeros_like(factors)) for i in range(QUAD)], axis=1)
        points = dot(jnp.concatenate([done[j, q] for q in range(4)], axis=1), factors, ((0,), (0,))).astype(BF16)
        for q in range(4):
            for b in range(2):
                row = (2 * q + b) * 64
                for i in range(QUAD):
                    out[g, i, 4 * q + 2 * h + b] = points[row:row + 64, i * 128:(i + 1) * 128]

    def settle(j):
        _, back, _ = sides(j)
        _, ring_from = ring_sides(j)
        sent = [far_copy(j), near_copy(j), sum_copy(j), ahead_copy(j, z), back_copy(j, z), on_copy(j, back),
                ring_ahead(j, me), ring_back(j, me), ring_on(j, ring_from)]
        for copy in sent:
            copy.wait_send()

        @pl.when(lax.rem(j, 2) == 1)
        def _():
            mid_copy(lax.div(j, 2)).wait_send()

    paired = (prepare, two_levels, last_level)
    stages = (leaf, pass_on, first_state, prepare, ring_hand_on, two_levels, last_level, hand_on, finish, settle)

    def step(s, carry):
        for at in ORDER:
            lag, stage = lags[at], stages[at]
            j = s - lag
            due = (j >= 0) & (j < chunks)
            if stage in paired:
                due = due & (lax.rem(j, 2) == 1)

            @pl.when(due)
            def _(stage=stage, j=j):
                stage(j)

        return carry

    lax.fori_loop(0, chunks + max(lags), step, 0)
    t_copy.wait_send()


def mixed(rows, cid, plan, x, v, t, u):
    batches, orders, fields, points = x.shape
    groups = orders // QUAD
    chunks = 2 * groups
    chunk = (chunks, rows, 128)
    smem, vmem, hbm = (pl.BlockSpec(memory_space=m) for m in (pltpu.SMEM, pltpu.VMEM, pltpu.HBM))
    x = x.reshape(4, 2, batches // 8, orders, fields, points)
    arrays = [
        *[(x.shape[2:], BF16)] * 8, (v.shape, BF16), (t.shape, BF16), (u.shape, BF16),
        ((rows, QUAD * 128), BF16), ((groups, rows, 128), BF16), ((4, groups, 2, rows, rows), BF16),
        *[(chunk, BF16)] * 6, *[(chunk, F32)] * 2,
        ((chunks, 4, rows, 128), BF16), *[((groups, 2, rows, 128), BF16)] * 2, ((chunks, 4, rows, 128), BF16),
        (t.shape[1:], BF16)]
    size = sum(math.prod(shape[:-1]) * -(-shape[-1] // 128) * 128 * jnp.dtype(kind).itemsize for shape, kind in arrays)
    return pl.pallas_call(
        functools.partial(mixing, rows, LAGS),
        out_shape=jax.ShapeDtypeStruct((groups, QUAD, batches, fields, points), BF16),
        in_specs=[smem, hbm, hbm, hbm, hbm],
        out_specs=vmem,
        scratch_shapes=[
            *[pltpu.VMEM(shape, kind) for shape, kind in arrays],
            pltpu.SemaphoreType.DMA((10, chunks)),
            pltpu.SemaphoreType.DMA((10, chunks)),
            pltpu.SemaphoreType.DMA,
            pltpu.SemaphoreType.DMA,
            pltpu.SemaphoreType.DMA((11,)),
        ],
        compiler_params=pltpu.CompilerParams(
            collective_id=cid, has_side_effects=True, vmem_limit_bytes=size + 13 * 2**20),
        cost_estimate=pl.CostEstimate(flops=10**9, bytes_accessed=16 * 2**20, transcendentals=0),
    )(plan, x, v, t, u)


def dealing(plan, packed, out, sem):
    groups = packed.shape[0]
    copies = [pltpu.make_async_copy(packed.at[g, i], out.at[:, plan[0, QUAD * g + i]], sem.at[g, i])
              for g in range(groups) for i in range(QUAD)]
    for copy in copies:
        copy.start()
    for copy in copies:
        copy.wait()


def dealt_out(plan, packed, shape):
    smem, vmem, hbm = (pl.BlockSpec(memory_space=m) for m in (pltpu.SMEM, pltpu.VMEM, pltpu.HBM))
    return pl.pallas_call(
        dealing,
        out_shape=jax.ShapeDtypeStruct(shape, BF16),
        in_specs=[smem, vmem],
        out_specs=hbm,
        scratch_shapes=[pltpu.SemaphoreType.DMA(packed.shape[:2])],
        compiler_params=pltpu.CompilerParams(vmem_limit_bytes=16 * 2**20),
    )(plan, packed)


def settled(result):
    anywhere = pl.BlockSpec(memory_space=pl.ANY)
    return pl.pallas_call(
        lambda given, out: None,
        out_shape=jax.ShapeDtypeStruct(result.shape, result.dtype),
        in_specs=[anywhere],
        out_specs=anywhere,
        input_output_aliases={0: 0},
    )(result)


def turned(row):
    n = row.shape[1]
    i, j = (lax.broadcasted_iota(I32, (n, n), d) for d in (0, 1))
    return jnp.sum(jnp.where(i == j, jnp.broadcast_to(row, (n, n)), 0.0), axis=1, keepdims=True)


def planning(heights, orders, ranks, plan, pick):
    n = ranks.shape[0]
    groups = n // QUAD
    i, j = (lax.broadcasted_iota(I32, (n, n), d).astype(F32) for d in (0, 1))
    lane = lax.broadcasted_iota(I32, (1, n), 1).astype(F32)
    rank = ranks[...].reshape(1, n).astype(F32)
    order = orders[...].reshape(1, n).astype(F32)
    rank_down, order_down = turned(rank), turned(order)
    ahead = (rank_down > rank) | ((rank_down == rank) & (i < j))
    spot = jnp.sum(jnp.where(ahead, 1.0, 0.0), axis=0, keepdims=True)
    turn = sum(jnp.where(spot >= groups * m, 1.0, 0.0) for m in range(1, QUAD))
    k = spot - groups * turn
    back = (turn == 1.0) | (turn == 3.0)
    slot = QUAD * jnp.where(back, groups - 1.0 - k, k) + turn
    here = turned(slot) == j

    def dealt(values):
        return jnp.sum(jnp.where(here, values, 0.0), axis=0, keepdims=True)

    rank_here = dealt(rank_down)
    group = sum(jnp.where(lane >= QUAD * m, 1.0, 0.0) for m in range(1, groups))
    earlier = (turned(group) == group) & (i < j)
    first = jnp.sum(jnp.where(earlier, turned(rank_here), 0.0), axis=0, keepdims=True)
    for at, row in enumerate((dealt(i), first, rank_here, dealt(order_down))):
        plan[at:at + 1, :] = row.astype(I32)
    most = jnp.max(first + rank_here)
    pick[0] = sum((most > height).astype(I32) for height in heights[:-1])


def planned(heights, orders, ranks):
    vmem, smem = (pl.BlockSpec(memory_space=m) for m in (pltpu.VMEM, pltpu.SMEM))
    return pl.pallas_call(
        functools.partial(planning, heights),
        out_shape=(jax.ShapeDtypeStruct((4, ranks.shape[0]), I32), jax.ShapeDtypeStruct((1,), I32)),
        in_specs=[vmem, vmem],
        out_specs=(vmem, smem),
    )(orders, ranks)


def shards(coefficients, v_factors, transfer, u_factors, orders, ranks):
    most = QUAD * v_factors.shape[1]
    heights = tuple(most * part // 16 for part in PARTS)
    plan, pick = planned(heights, orders, ranks)

    def branch(rows, cid, plan, x, v, t, u):
        return dealt_out(plan, mixed(rows, cid, plan, x, v, t, u), x.shape)

    branches = [functools.partial(branch, rows, 1 + at) for at, rows in enumerate(heights)]
    return settled(lax.switch(pick[0], branches, plan, coefficients, v_factors, transfer, u_factors))


def solution(mesh):
    placed = (
        P(None, None, None, ("col", "rank")),
        P(None, None, ("col", "rank")),
        P(None, None, "col", None, None),
        P(None, None, ("col", "rank")),
        P(),
        P(),
    )
    return jax.shard_map(
        shards,
        mesh=mesh,
        in_specs=placed,
        out_specs=P(None, None, None, ("col", "rank")),
        check_vma=False,
    )
```

```python
import functools
import math

import jax
import jax.numpy as jnp
from jax import lax
from jax.experimental import pallas as pl
from jax.experimental.pallas import tpu as pltpu
from jax.sharding import PartitionSpec as P

MESH = pl.DeviceIdType.MESH
BF16, F32, I32 = jnp.bfloat16, jnp.float32, jnp.int32
QUAD = 4
LAGS = (0, 4, 8, 13, 11, 14, 18, 22, 26, 27)
ORDER = (0, 7, 6, 5, 4, 2, 1, 3, 8, 9)
PARTS = (10, 11, 12, 16)


def dot(a, b, dims=((1,), (0,))):
    return lax.dot_general(a, b, (dims, ((), ())), preferred_element_type=F32)


def spots(plan, g):
    first = [plan[1, QUAD * g + i] for i in range(QUAD)]
    rank = [plan[2, QUAD * g + i] for i in range(QUAD)]
    return first, rank, first[QUAD - 1] + rank[QUAD - 1]


def placing(plan, g, rows, width):
    first, rank, _ = spots(plan, g)
    lane = lax.broadcasted_iota(I32, (1, QUAD * width), 1)
    target = jnp.full((1, QUAD * width), -1, I32)
    for i in range(QUAD):
        k = lane - i * width
        here = (k >= 0) & (k < rank[i])
        target = jnp.where(here, first[i] + k, target)
    row = lax.broadcasted_iota(I32, (rows, QUAD * width), 0)
    return jnp.where(row == target, 1.0, 0.0).astype(BF16)


def order_of(plan, g, index):
    first, _, _ = spots(plan, g)
    seg = jnp.zeros(index.shape, I32)
    for i in range(1, QUAD):
        seg = seg + jnp.where(index >= first[i], 1, 0)
    return seg


def mixing(rows, lags, plan, x_hbm, v_hbm, t_hbm, u_hbm, out, *scratch):
    *x, v, t, u, a, u_packed, maps, far, far_in, near, near_in, summed, summed_in, keep_next, keep_own, blocks, mid, mid_in, \
        done, t_in, send, recv, t_send, t_recv, load_sem = scratch
    col, z = lax.axis_index("col"), lax.axis_index("rank")
    n_col = lax.axis_size("col")
    stride = n_col // 4
    me = lax.div(col, stride)
    half = stride // 2
    width = v.shape[1]
    chunks = done.shape[0]

    def at(step):
        return lax.rem(z + step, 4)

    def ring(step):
        return lax.rem(me + step, 4)

    def block(place):
        return place * stride + lax.rem(col, stride)

    pair = me + 1 - 2 * lax.rem(me, 2)
    opposite = ring(2)
    pair_opposite = lax.rem(pair + 2, 4)
    last = col + half - 2 * half * lax.rem(lax.div(col, half), 2)

    quarters = [(at(2), at(3 - 2 * h), at(1 + 2 * h), z) for h in range(2)]
    x_loads = [(x_hbm.at[q, h], x[4 * h + i]) for h in range(2) for i, q in enumerate(quarters[h])]
    loads = [pltpu.make_async_copy(src, dst, load_sem.at[i])
             for i, (src, dst) in enumerate([(v_hbm, v), *x_loads, (t_hbm, t), (u_hbm, u)])]
    for load in loads:
        load.start()

    peers = [(col, at(1)), (col, at(3)), (block(ring(1)), z), (block(ring(3)), z), (last, z)]
    barrier = pltpu.get_barrier_semaphore()
    for peer in peers:
        pl.semaphore_signal(barrier, inc=1, device_id=peer, device_id_type=MESH)
    pl.semaphore_wait(barrier, len(peers))

    t_copy = pltpu.make_async_remote_copy(
        src_ref=t_hbm.at[0], dst_ref=t_in, send_sem=t_send, recv_sem=t_recv,
        device_id=(block(pair), z), device_id_type=MESH)
    t_copy.start()

    def remote(kind, j, src, dst, peer):
        return pltpu.make_async_remote_copy(
            src_ref=src, dst_ref=dst, send_sem=send.at[kind, j], recv_sem=recv.at[kind, j],
            device_id=peer, device_id_type=MESH)

    def sides(j):
        h = lax.rem(j, 2)
        return at(1 + 2 * h), at(3 - 2 * h), at(2)

    def ring_sides(j):
        h = lax.rem(j, 2)
        return ring(1 + 2 * h), ring(3 - 2 * h)

    def far_copy(j):
        ahead, _, _ = sides(j)
        return remote(0, j, far.at[j], far_in.at[j], (col, ahead))

    def near_copy(j):
        _, back, _ = sides(j)
        return remote(1, j, near.at[j], near_in.at[j], (col, back))

    def sum_copy(j):
        ahead, _, _ = sides(j)
        return remote(2, j, summed.at[j], summed_in.at[j], (col, ahead))

    def ahead_copy(j, q):
        ahead, _, _ = sides(j)
        return remote(3, j, done.at[j, q], done.at[j, q], (col, ahead))

    def back_copy(j, q):
        _, back, _ = sides(j)
        return remote(4, j, done.at[j, q], done.at[j, q], (col, back))

    def on_copy(j, q):
        ahead, _, _ = sides(j)
        return remote(5, j, done.at[j, q], done.at[j, q], (col, ahead))

    def ring_ahead(j, c):
        ahead, _ = ring_sides(j)
        return remote(6, j, blocks.at[j, c], blocks.at[j, c], (block(ahead), z))

    def ring_back(j, c):
        _, back = ring_sides(j)
        return remote(7, j, blocks.at[j, c], blocks.at[j, c], (block(back), z))

    def ring_on(j, c):
        ahead, _ = ring_sides(j)
        return remote(8, j, blocks.at[j, c], blocks.at[j, c], (block(ahead), z))

    def mid_copy(j):
        return remote(9, j, mid.at[j], mid_in.at[j], (last, z))

    def leaf(j):
        g, h = lax.div(j, 2), lax.rem(j, 2)

        def halved(half):
            parts = x[4 * half:4 * half + 4]

            def fields(part):
                return jnp.concatenate([
                    jnp.concatenate([part[b, plan[0, QUAD * g + i]] for i in range(QUAD)], axis=1)
                    for b in range(2)], axis=0)

            def leaves(at):
                @pl.when(j == half)
                def _():
                    loads[1 + 4 * half + at].wait()
                    loads[2 + 4 * half + at].wait()

                return dot(a[...], jnp.concatenate([fields(parts[at]), fields(parts[at + 1])], axis=0), ((1,), (1,)))

            sent = leaves(0)
            far[j] = sent[:, :128].astype(BF16)
            near[j] = sent[:, 128:].astype(BF16)
            far_copy(j).start()
            near_copy(j).start()
            kept = leaves(2)
            keep_next[j] = kept[:, :128]
            keep_own[j] = kept[:, 128:]

        @pl.when(j == 0)
        def _():
            loads[0].wait()

        @pl.when(h == 0)
        def _():
            first, _, _ = spots(plan, g)
            packed = dot(placing(plan, g, rows, width),
                         jnp.concatenate([v[plan[0, QUAD * g + i]] for i in range(QUAD)], axis=0))
            seg = order_of(plan, g, lax.broadcasted_iota(I32, (rows, 1), 0))
            degree = (col * 4 + z) * 128 + lax.broadcasted_iota(I32, (1, 128), 1)
            for i in range(QUAD):
                kept = (seg == i) & (degree >= plan[3, QUAD * g + i])
                a[:, i * 128:(i + 1) * 128] = jnp.where(kept, packed, 0.0).astype(BF16)

        @pl.when(h == 0)
        def _():
            halved(0)

        @pl.when(h == 1)
        def _():
            halved(1)

    def prepare(j):
        g = lax.div(j, 2)

        @pl.when(j == 1)
        def _():
            loads[9].wait()
            loads[10].wait()
            t_copy.wait_recv()

        first, _, filled = spots(plan, g)
        lane = lax.broadcasted_iota(I32, (1, rows), 1)
        seg = order_of(plan, g, lane)
        k = lane
        for i in range(1, QUAD):
            k = jnp.where(seg == i, lane - first[i], k)
        k = jnp.where(lane < filled, k, -1000)
        j_row = lax.broadcasted_iota(I32, (2 * width, rows), 0)
        pick_own = jnp.where(j_row == k, 1.0, 0.0).astype(BF16)
        pick_partner = jnp.where(j_row - width == k, 1.0, 0.0).astype(BF16)
        row = lax.broadcasted_iota(I32, (rows, 1), 0)
        same = order_of(plan, g, row) == seg
        p = placing(plan, g, rows, width)
        u_packed[g] = dot(p, jnp.concatenate([u[plan[0, QUAD * g + i]] for i in range(QUAD)], axis=0)).astype(BF16)
        reads = [lambda o: t[0, o, 0], lambda o: t_in[o, 0], lambda o: t[1, o, 0], lambda o: t[2, o, 0]]
        parts = []
        for m in range(0, 4, 2):
            stack = jnp.concatenate([
                jnp.concatenate([read(plan[0, QUAD * g + i]) for read in reads[m:m + 2]], axis=1)
                for i in range(QUAD)], axis=0)
            packed = dot(p, stack).astype(BF16)
            parts += [packed[:, :2 * width], packed[:, 2 * width:]]
        parts = jnp.concatenate(parts, axis=0)
        for side, pick in enumerate((pick_own, pick_partner)):
            placed = dot(parts, pick)
            for m in range(4):
                maps[m, g, side] = jnp.where(same, placed[m * rows:(m + 1) * rows], 0.0).astype(BF16)

    def pass_on(j):
        far_copy(j).wait_recv()
        summed[j] = (keep_next[j] + far_in[j].astype(F32)).astype(BF16)
        sum_copy(j).start()

    def first_state(j):
        near_copy(j).wait_recv()
        sum_copy(j).wait_recv()
        total = keep_own[j] + near_in[j].astype(F32) + summed_in[j].astype(F32)
        blocks[j, me] = total.astype(BF16)
        ring_ahead(j, me).start()
        ring_back(j, me).start()

    def ring_hand_on(j):
        _, back = ring_sides(j)
        ring_ahead(j, back).wait_recv()
        ring_on(j, back).start()

    def mix(m, g, own, partner):
        return (dot(maps[m, g, 0], own) + dot(maps[m, g, 1], partner)).astype(BF16)

    def two_levels(j):
        g = lax.div(j, 2)
        for c in (j - 1, j):
            ahead, _ = ring_sides(c)
            ring_back(c, ahead).wait_recv()
            ring_on(c, opposite).wait_recv()

        def both(c):
            return jnp.concatenate([blocks[j - 1, c], blocks[j, c]], axis=1)

        own = mix(0, g, both(me), both(opposite))
        partner = mix(1, g, both(pair), both(pair_opposite))
        new = mix(2, g, own, partner)
        mid[g, 0] = new[:, :128]
        mid[g, 1] = new[:, 128:]
        mid_copy(g).start()

    def last_level(j):
        g = lax.div(j, 2)
        mid_copy(g).wait_recv()
        new = mix(3, g, jnp.concatenate([mid[g, 0], mid[g, 1]], axis=1),
                  jnp.concatenate([mid_in[g, 0], mid_in[g, 1]], axis=1))
        for n, c in enumerate((j - 1, j)):
            done[c, z] = new[:, n * 128:(n + 1) * 128]
            ahead_copy(c, z).start()
            back_copy(c, z).start()

    def hand_on(j):
        _, back, _ = sides(j)
        ahead_copy(j, back).wait_recv()
        on_copy(j, back).start()

    def finish(j):
        ahead, _, across = sides(j)
        back_copy(j, ahead).wait_recv()
        on_copy(j, across).wait_recv()
        g, h = lax.div(j, 2), lax.rem(j, 2)
        seg = order_of(plan, g, lax.broadcasted_iota(I32, (rows, 1), 0))
        factors = u_packed[g]
        factors = jnp.concatenate([jnp.where(seg == i, factors, jnp.zeros_like(factors)) for i in range(QUAD)], axis=1)
        points = dot(jnp.concatenate([done[j, q] for q in range(4)], axis=1), factors, ((0,), (0,))).astype(BF16)
        for q in range(4):
            for b in range(2):
                row = (2 * q + b) * 64
                for i in range(QUAD):
                    out[g, i, 4 * q + 2 * h + b] = points[row:row + 64, i * 128:(i + 1) * 128]

    def settle(j):
        _, back, _ = sides(j)
        _, ring_from = ring_sides(j)
        sent = [far_copy(j), near_copy(j), sum_copy(j), ahead_copy(j, z), back_copy(j, z), on_copy(j, back),
                ring_ahead(j, me), ring_back(j, me), ring_on(j, ring_from)]
        for copy in sent:
            copy.wait_send()

        @pl.when(lax.rem(j, 2) == 1)
        def _():
            mid_copy(lax.div(j, 2)).wait_send()

    paired = (prepare, two_levels, last_level)
    stages = (leaf, pass_on, first_state, prepare, ring_hand_on, two_levels, last_level, hand_on, finish, settle)

    def step(s, carry):
        for at in ORDER:
            lag, stage = lags[at], stages[at]
            j = s - lag
            due = (j >= 0) & (j < chunks)
            if stage in paired:
                due = due & (lax.rem(j, 2) == 1)

            @pl.when(due)
            def _(stage=stage, j=j):
                stage(j)

        return carry

    lax.fori_loop(0, chunks + max(lags), step, 0)
    t_copy.wait_send()


def mixed(rows, cid, plan, x, v, t, u):
    batches, orders, fields, points = x.shape
    groups = orders // QUAD
    chunks = 2 * groups
    chunk = (chunks, rows, 128)
    smem, vmem, hbm = (pl.BlockSpec(memory_space=m) for m in (pltpu.SMEM, pltpu.VMEM, pltpu.HBM))
    x = x.reshape(4, 2, batches // 8, orders, fields, points)
    arrays = [
        *[(x.shape[2:], BF16)] * 8, (v.shape, BF16), (t.shape, BF16), (u.shape, BF16),
        ((rows, QUAD * 128), BF16), ((groups, rows, 128), BF16), ((4, groups, 2, rows, rows), BF16),
        *[(chunk, BF16)] * 6, *[(chunk, F32)] * 2,
        ((chunks, 4, rows, 128), BF16), *[((groups, 2, rows, 128), BF16)] * 2, ((chunks, 4, rows, 128), BF16),
        (t.shape[1:], BF16)]
    size = sum(math.prod(shape[:-1]) * -(-shape[-1] // 128) * 128 * jnp.dtype(kind).itemsize for shape, kind in arrays)
    return pl.pallas_call(
        functools.partial(mixing, rows, LAGS),
        out_shape=jax.ShapeDtypeStruct((groups, QUAD, batches, fields, points), BF16),
        in_specs=[smem, hbm, hbm, hbm, hbm],
        out_specs=vmem,
        scratch_shapes=[
            *[pltpu.VMEM(shape, kind) for shape, kind in arrays],
            pltpu.SemaphoreType.DMA((10, chunks)),
            pltpu.SemaphoreType.DMA((10, chunks)),
            pltpu.SemaphoreType.DMA,
            pltpu.SemaphoreType.DMA,
            pltpu.SemaphoreType.DMA((11,)),
        ],
        compiler_params=pltpu.CompilerParams(
            collective_id=cid, has_side_effects=True, vmem_limit_bytes=size + 13 * 2**20),
        cost_estimate=pl.CostEstimate(flops=10**9, bytes_accessed=16 * 2**20, transcendentals=0),
    )(plan, x, v, t, u)


def dealing(plan, packed, out, sem):
    groups = packed.shape[0]
    copies = [pltpu.make_async_copy(packed.at[g, i], out.at[:, plan[0, QUAD * g + i]], sem.at[g, i])
              for g in range(groups) for i in range(QUAD)]
    for copy in copies:
        copy.start()
    for copy in copies:
        copy.wait()


def dealt_out(plan, packed, shape):
    smem, vmem, hbm = (pl.BlockSpec(memory_space=m) for m in (pltpu.SMEM, pltpu.VMEM, pltpu.HBM))
    return pl.pallas_call(
        dealing,
        out_shape=jax.ShapeDtypeStruct(shape, BF16),
        in_specs=[smem, vmem],
        out_specs=hbm,
        scratch_shapes=[pltpu.SemaphoreType.DMA(packed.shape[:2])],
        compiler_params=pltpu.CompilerParams(vmem_limit_bytes=16 * 2**20),
    )(plan, packed)


def settled(result):
    anywhere = pl.BlockSpec(memory_space=pl.ANY)
    return pl.pallas_call(
        lambda given, out: None,
        out_shape=jax.ShapeDtypeStruct(result.shape, result.dtype),
        in_specs=[anywhere],
        out_specs=anywhere,
        input_output_aliases={0: 0},
    )(result)


def turned(row):
    n = row.shape[1]
    i, j = (lax.broadcasted_iota(I32, (n, n), d) for d in (0, 1))
    return jnp.sum(jnp.where(i == j, jnp.broadcast_to(row, (n, n)), 0.0), axis=1, keepdims=True)


def planning(heights, orders, ranks, plan, pick):
    n = ranks.shape[0]
    groups = n // QUAD
    i, j = (lax.broadcasted_iota(I32, (n, n), d).astype(F32) for d in (0, 1))
    rank = ranks[...].reshape(1, n).astype(F32)
    order = orders[...].reshape(1, n).astype(F32)
    rank_down, order_down = turned(rank), turned(order)
    ahead = (rank_down > rank) | ((rank_down == rank) & (i < j))
    spot = jnp.sum(jnp.where(ahead, 1.0, 0.0), axis=0, keepdims=True)
    turn = sum(jnp.where(spot >= groups * m, 1.0, 0.0) for m in range(1, QUAD))
    k = spot - groups * turn
    back = (turn == 1.0) | (turn == 3.0)
    slot = QUAD * jnp.where(back, groups - 1.0 - k, k) + turn
    here = turned(slot) == j

    def dealt(values):
        return jnp.sum(jnp.where(here, values, 0.0), axis=0, keepdims=True)

    rank_here = dealt(rank_down)
    group, group_down = (sum(jnp.where(at >= QUAD * m, 1.0, 0.0) for m in range(1, groups)) for at in (j, i))
    rank_here_down = jnp.sum(jnp.where(slot == i, rank, 0.0), axis=1, keepdims=True)
    first = jnp.sum(jnp.where((group_down == group) & (i < j), rank_here_down, 0.0), axis=0, keepdims=True)
    for at, row in enumerate((dealt(i), first, rank_here, dealt(order_down))):
        plan[at:at + 1, :] = row.astype(I32)
    most = jnp.max(first + rank_here)
    pick[0] = sum((most > height).astype(I32) for height in heights[:-1])


def planned(heights, orders, ranks):
    vmem, smem = (pl.BlockSpec(memory_space=m) for m in (pltpu.VMEM, pltpu.SMEM))
    return pl.pallas_call(
        functools.partial(planning, heights),
        out_shape=(jax.ShapeDtypeStruct((4, ranks.shape[0]), I32), jax.ShapeDtypeStruct((1,), I32)),
        in_specs=[vmem, vmem],
        out_specs=(vmem, smem),
    )(orders, ranks)


def shards(coefficients, v_factors, transfer, u_factors, orders, ranks):
    most = QUAD * v_factors.shape[1]
    heights = tuple(most * part // 16 for part in PARTS)
    plan, pick = planned(heights, orders, ranks)

    def branch(rows, cid, plan, x, v, t, u):
        return dealt_out(plan, mixed(rows, cid, plan, x, v, t, u), x.shape)

    branches = [functools.partial(branch, rows, 1 + at) for at, rows in enumerate(heights)]
    return settled(lax.switch(pick[0], branches, plan, coefficients, v_factors, transfer, u_factors))


def solution(mesh):
    placed = (
        P(None, None, None, ("col", "rank")),
        P(None, None, ("col", "rank")),
        P(None, None, "col", None, None),
        P(None, None, ("col", "rank")),
        P(),
        P(),
    )
    return jax.shard_map(
        shards,
        mesh=mesh,
        in_specs=placed,
        out_specs=P(None, None, None, ("col", "rank")),
        check_vma=False,
    )
```

```python
import functools
import math

import jax
import jax.numpy as jnp
from jax import lax
from jax.experimental import pallas as pl
from jax.experimental.pallas import tpu as pltpu
from jax.sharding import PartitionSpec as P

MESH = pl.DeviceIdType.MESH
BF16, F32, I32 = jnp.bfloat16, jnp.float32, jnp.int32
QUAD = 4
LAGS = (0, 4, 8, 13, 11, 14, 18, 22, 26, 27)
ORDER = (0, 7, 6, 5, 4, 2, 1, 3, 8, 9)
PARTS = (10, 11, 12, 16)


def dot(a, b, dims=((1,), (0,))):
    return lax.dot_general(a, b, (dims, ((), ())), preferred_element_type=F32)


def spots(plan, g):
    first = [plan[1, QUAD * g + i] for i in range(QUAD)]
    rank = [plan[2, QUAD * g + i] for i in range(QUAD)]
    return first, rank, first[QUAD - 1] + rank[QUAD - 1]


def placing(plan, g, rows, width):
    first, rank, _ = spots(plan, g)
    lane = lax.broadcasted_iota(I32, (1, QUAD * width), 1)
    target = jnp.full((1, QUAD * width), -1, I32)
    for i in range(QUAD):
        k = lane - i * width
        here = (k >= 0) & (k < rank[i])
        target = jnp.where(here, first[i] + k, target)
    row = lax.broadcasted_iota(I32, (rows, QUAD * width), 0)
    return jnp.where(row == target, 1.0, 0.0).astype(BF16)


def order_of(plan, g, index):
    first, _, _ = spots(plan, g)
    seg = jnp.zeros(index.shape, I32)
    for i in range(1, QUAD):
        seg = seg + jnp.where(index >= first[i], 1, 0)
    return seg


def mixing(rows, lags, plan, x_hbm, v_hbm, t_hbm, u_hbm, out, *scratch):
    *x, v, t, u, a, u_packed, maps, far, far_in, near, near_in, summed, summed_in, keep_next, keep_own, blocks, mid, mid_in, \
        done, t_in, send, recv, t_send, t_recv, load_sem = scratch
    col, z = lax.axis_index("col"), lax.axis_index("rank")
    n_col = lax.axis_size("col")
    stride = n_col // 4
    me = lax.div(col, stride)
    half = stride // 2
    width = v.shape[1]
    chunks = done.shape[0]

    def at(step):
        return lax.rem(z + step, 4)

    def ring(step):
        return lax.rem(me + step, 4)

    def block(place):
        return place * stride + lax.rem(col, stride)

    pair = me + 1 - 2 * lax.rem(me, 2)
    opposite = ring(2)
    pair_opposite = lax.rem(pair + 2, 4)
    last = col + half - 2 * half * lax.rem(lax.div(col, half), 2)

    quarters = [(at(2), at(3 - 2 * h), at(1 + 2 * h), z) for h in range(2)]
    x_loads = [(x_hbm.at[q, h], x[4 * h + i]) for h in range(2) for i, q in enumerate(quarters[h])]
    loads = [pltpu.make_async_copy(src, dst, load_sem.at[i])
             for i, (src, dst) in enumerate([(v_hbm, v), *x_loads, (t_hbm, t), (u_hbm, u)])]
    for load in loads:
        load.start()

    peers = [(col, at(1)), (col, at(3)), (block(ring(1)), z), (block(ring(3)), z), (last, z)]
    barrier = pltpu.get_barrier_semaphore()
    for peer in peers:
        pl.semaphore_signal(barrier, inc=1, device_id=peer, device_id_type=MESH)
    pl.semaphore_wait(barrier, len(peers))

    t_copy = pltpu.make_async_remote_copy(
        src_ref=t_hbm.at[0], dst_ref=t_in, send_sem=t_send, recv_sem=t_recv,
        device_id=(block(pair), z), device_id_type=MESH)
    t_copy.start()

    def remote(kind, j, src, dst, peer):
        return pltpu.make_async_remote_copy(
            src_ref=src, dst_ref=dst, send_sem=send.at[kind, j], recv_sem=recv.at[kind, j],
            device_id=peer, device_id_type=MESH)

    def sides(j):
        h = lax.rem(j, 2)
        return at(1 + 2 * h), at(3 - 2 * h), at(2)

    def ring_sides(j):
        h = lax.rem(j, 2)
        return ring(1 + 2 * h), ring(3 - 2 * h)

    def far_copy(j):
        ahead, _, _ = sides(j)
        return remote(0, j, far.at[j], far_in.at[j], (col, ahead))

    def near_copy(j):
        _, back, _ = sides(j)
        return remote(1, j, near.at[j], near_in.at[j], (col, back))

    def sum_copy(j):
        ahead, _, _ = sides(j)
        return remote(2, j, summed.at[j], summed_in.at[j], (col, ahead))

    def ahead_copy(j, q):
        ahead, _, _ = sides(j)
        return remote(3, j, done.at[j, q], done.at[j, q], (col, ahead))

    def back_copy(j, q):
        _, back, _ = sides(j)
        return remote(4, j, done.at[j, q], done.at[j, q], (col, back))

    def on_copy(j, q):
        ahead, _, _ = sides(j)
        return remote(5, j, done.at[j, q], done.at[j, q], (col, ahead))

    def ring_ahead(j, c):
        ahead, _ = ring_sides(j)
        return remote(6, j, blocks.at[j, c], blocks.at[j, c], (block(ahead), z))

    def ring_back(j, c):
        _, back = ring_sides(j)
        return remote(7, j, blocks.at[j, c], blocks.at[j, c], (block(back), z))

    def ring_on(j, c):
        ahead, _ = ring_sides(j)
        return remote(8, j, blocks.at[j, c], blocks.at[j, c], (block(ahead), z))

    def mid_copy(j):
        return remote(9, j, mid.at[j], mid_in.at[j], (last, z))

    def leaf(j):
        g, h = lax.div(j, 2), lax.rem(j, 2)

        def halved(half):
            parts = x[4 * half:4 * half + 4]

            def fields(part):
                return jnp.concatenate([
                    jnp.concatenate([part[b, plan[0, QUAD * g + i]] for i in range(QUAD)], axis=1)
                    for b in range(2)], axis=0)

            def leaves(at):
                @pl.when(j == half)
                def _():
                    loads[1 + 4 * half + at].wait()
                    loads[2 + 4 * half + at].wait()

                return dot(a[...], jnp.concatenate([fields(parts[at]), fields(parts[at + 1])], axis=0), ((1,), (1,)))

            sent = leaves(0)
            far[j] = sent[:, :128].astype(BF16)
            near[j] = sent[:, 128:].astype(BF16)
            far_copy(j).start()
            near_copy(j).start()
            kept = leaves(2)
            keep_next[j] = kept[:, :128]
            keep_own[j] = kept[:, 128:]

        @pl.when(j == 0)
        def _():
            loads[0].wait()

        @pl.when(h == 0)
        def _():
            first, _, _ = spots(plan, g)
            packed = dot(placing(plan, g, rows, width),
                         jnp.concatenate([v[plan[0, QUAD * g + i]] for i in range(QUAD)], axis=0))
            seg = order_of(plan, g, lax.broadcasted_iota(I32, (rows, 1), 0))
            degree = (col * 4 + z) * 128 + lax.broadcasted_iota(I32, (1, 128), 1)
            for i in range(QUAD):
                kept = (seg == i) & (degree >= plan[3, QUAD * g + i])
                a[:, i * 128:(i + 1) * 128] = jnp.where(kept, packed, 0.0).astype(BF16)

        @pl.when(h == 0)
        def _():
            halved(0)

        @pl.when(h == 1)
        def _():
            halved(1)

    def prepare(j):
        g = lax.div(j, 2)

        @pl.when(j == 1)
        def _():
            loads[9].wait()
            loads[10].wait()
            t_copy.wait_recv()

        first, _, filled = spots(plan, g)
        lane = lax.broadcasted_iota(I32, (1, rows), 1)
        seg = order_of(plan, g, lane)
        k = lane
        for i in range(1, QUAD):
            k = jnp.where(seg == i, lane - first[i], k)
        k = jnp.where(lane < filled, k, -1000)
        j_row = lax.broadcasted_iota(I32, (2 * width, rows), 0)
        pick_own = jnp.where(j_row == k, 1.0, 0.0).astype(BF16)
        pick_partner = jnp.where(j_row - width == k, 1.0, 0.0).astype(BF16)
        row = lax.broadcasted_iota(I32, (rows, 1), 0)
        same = order_of(plan, g, row) == seg
        p = placing(plan, g, rows, width)
        u_packed[g] = dot(p, jnp.concatenate([u[plan[0, QUAD * g + i]] for i in range(QUAD)], axis=0)).astype(BF16)
        reads = [lambda o: t[0, o, 0], lambda o: t_in[o, 0], lambda o: t[1, o, 0], lambda o: t[2, o, 0]]
        parts = []
        for m in range(0, 4, 2):
            stack = jnp.concatenate([
                jnp.concatenate([read(plan[0, QUAD * g + i]) for read in reads[m:m + 2]], axis=1)
                for i in range(QUAD)], axis=0)
            packed = dot(p, stack).astype(BF16)
            parts += [packed[:, :2 * width], packed[:, 2 * width:]]
        parts = jnp.concatenate(parts, axis=0)
        for side, pick in enumerate((pick_own, pick_partner)):
            placed = dot(parts, pick)
            for m in range(4):
                maps[m, g, side] = jnp.where(same, placed[m * rows:(m + 1) * rows], 0.0).astype(BF16)

    def pass_on(j):
        far_copy(j).wait_recv()
        summed[j] = (keep_next[j] + far_in[j].astype(F32)).astype(BF16)
        sum_copy(j).start()

    def first_state(j):
        near_copy(j).wait_recv()
        sum_copy(j).wait_recv()
        total = keep_own[j] + near_in[j].astype(F32) + summed_in[j].astype(F32)
        blocks[j, me] = total.astype(BF16)
        ring_ahead(j, me).start()
        ring_back(j, me).start()

    def ring_hand_on(j):
        _, back = ring_sides(j)
        ring_ahead(j, back).wait_recv()
        ring_on(j, back).start()

    def mix(m, g, own, partner):
        return (dot(maps[m, g, 0], own) + dot(maps[m, g, 1], partner)).astype(BF16)

    def two_levels(j):
        g = lax.div(j, 2)
        for c in (j - 1, j):
            ahead, _ = ring_sides(c)
            ring_back(c, ahead).wait_recv()
            ring_on(c, opposite).wait_recv()

        def both(c):
            return jnp.concatenate([blocks[j - 1, c], blocks[j, c]], axis=1)

        own = mix(0, g, both(me), both(opposite))
        partner = mix(1, g, both(pair), both(pair_opposite))
        new = mix(2, g, own, partner)
        mid[g, 0] = new[:, :128]
        mid[g, 1] = new[:, 128:]
        mid_copy(g).start()

    def last_level(j):
        g = lax.div(j, 2)
        mid_copy(g).wait_recv()
        new = mix(3, g, jnp.concatenate([mid[g, 0], mid[g, 1]], axis=1),
                  jnp.concatenate([mid_in[g, 0], mid_in[g, 1]], axis=1))
        for n, c in enumerate((j - 1, j)):
            done[c, z] = new[:, n * 128:(n + 1) * 128]
            ahead_copy(c, z).start()
            back_copy(c, z).start()

    def hand_on(j):
        _, back, _ = sides(j)
        ahead_copy(j, back).wait_recv()
        on_copy(j, back).start()

    def finish(j):
        ahead, _, across = sides(j)
        back_copy(j, ahead).wait_recv()
        on_copy(j, across).wait_recv()
        g, h = lax.div(j, 2), lax.rem(j, 2)
        seg = order_of(plan, g, lax.broadcasted_iota(I32, (rows, 1), 0))
        factors = u_packed[g]
        factors = jnp.concatenate([jnp.where(seg == i, factors, jnp.zeros_like(factors)) for i in range(QUAD)], axis=1)
        points = dot(jnp.concatenate([done[j, q] for q in range(4)], axis=1), factors, ((0,), (0,))).astype(BF16)
        for q in range(4):
            for b in range(2):
                row = (2 * q + b) * 64
                for i in range(QUAD):
                    out[g, i, 4 * q + 2 * h + b] = points[row:row + 64, i * 128:(i + 1) * 128]

    def settle(j):
        _, back, _ = sides(j)
        _, ring_from = ring_sides(j)
        sent = [far_copy(j), near_copy(j), sum_copy(j), ahead_copy(j, z), back_copy(j, z), on_copy(j, back),
                ring_ahead(j, me), ring_back(j, me), ring_on(j, ring_from)]
        for copy in sent:
            copy.wait_send()

        @pl.when(lax.rem(j, 2) == 1)
        def _():
            mid_copy(lax.div(j, 2)).wait_send()

    paired = (prepare, two_levels, last_level)
    stages = (leaf, pass_on, first_state, prepare, ring_hand_on, two_levels, last_level, hand_on, finish, settle)

    def step(s, carry):
        for at in ORDER:
            lag, stage = lags[at], stages[at]
            j = s - lag
            due = (j >= 0) & (j < chunks)
            if stage in paired:
                due = due & (lax.rem(j, 2) == 1)

            @pl.when(due)
            def _(stage=stage, j=j):
                stage(j)

        return carry

    lax.fori_loop(0, chunks + max(lags), step, 0)
    t_copy.wait_send()


def mixed(rows, cid, plan, x, v, t, u):
    batches, orders, fields, points = x.shape
    groups = orders // QUAD
    chunks = 2 * groups
    chunk = (chunks, rows, 128)
    smem, vmem, hbm = (pl.BlockSpec(memory_space=m) for m in (pltpu.SMEM, pltpu.VMEM, pltpu.HBM))
    x = x.reshape(4, 2, batches // 8, orders, fields, points)
    arrays = [
        *[(x.shape[2:], BF16)] * 8, (v.shape, BF16), (t.shape, BF16), (u.shape, BF16),
        ((rows, QUAD * 128), BF16), ((groups, rows, 128), BF16), ((4, groups, 2, rows, rows), BF16),
        *[(chunk, BF16)] * 6, *[(chunk, F32)] * 2,
        ((chunks, 4, rows, 128), BF16), *[((groups, 2, rows, 128), BF16)] * 2, ((chunks, 4, rows, 128), BF16),
        (t.shape[1:], BF16)]
    size = sum(math.prod(shape[:-1]) * -(-shape[-1] // 128) * 128 * jnp.dtype(kind).itemsize for shape, kind in arrays)
    return pl.pallas_call(
        functools.partial(mixing, rows, LAGS),
        out_shape=jax.ShapeDtypeStruct((groups, QUAD, batches, fields, points), BF16),
        in_specs=[smem, hbm, hbm, hbm, hbm],
        out_specs=vmem,
        scratch_shapes=[
            *[pltpu.VMEM(shape, kind) for shape, kind in arrays],
            pltpu.SemaphoreType.DMA((10, chunks)),
            pltpu.SemaphoreType.DMA((10, chunks)),
            pltpu.SemaphoreType.DMA,
            pltpu.SemaphoreType.DMA,
            pltpu.SemaphoreType.DMA((11,)),
        ],
        compiler_params=pltpu.CompilerParams(
            collective_id=cid, has_side_effects=True, vmem_limit_bytes=size + 13 * 2**20),
        cost_estimate=pl.CostEstimate(flops=10**9, bytes_accessed=16 * 2**20, transcendentals=0),
    )(plan, x, v, t, u)


def dealing(plan, packed, out, sem):
    groups = packed.shape[0]
    copies = [pltpu.make_async_copy(packed.at[g, i], out.at[:, plan[0, QUAD * g + i]], sem.at[g, i])
              for g in range(groups) for i in range(QUAD)]
    for copy in copies:
        copy.start()
    for copy in copies:
        copy.wait()


def dealt_out(plan, packed, shape):
    smem, vmem, hbm = (pl.BlockSpec(memory_space=m) for m in (pltpu.SMEM, pltpu.VMEM, pltpu.HBM))
    return pl.pallas_call(
        dealing,
        out_shape=jax.ShapeDtypeStruct(shape, BF16),
        in_specs=[smem, vmem],
        out_specs=hbm,
        scratch_shapes=[pltpu.SemaphoreType.DMA(packed.shape[:2])],
        compiler_params=pltpu.CompilerParams(vmem_limit_bytes=16 * 2**20),
    )(plan, packed)


def settled(result):
    anywhere = pl.BlockSpec(memory_space=pl.ANY)
    return pl.pallas_call(
        lambda given, out: None,
        out_shape=jax.ShapeDtypeStruct(result.shape, result.dtype),
        in_specs=[anywhere],
        out_specs=anywhere,
        input_output_aliases={0: 0},
    )(result)


def turned(row):
    n = row.shape[1]
    i, j = (lax.broadcasted_iota(I32, (n, n), d) for d in (0, 1))
    return jnp.sum(jnp.where(i == j, jnp.broadcast_to(row, (n, n)), 0.0), axis=1, keepdims=True)


def planning(heights, orders, ranks, plan, pick):
    n = ranks.shape[0]
    groups = n // QUAD
    i, j = (lax.broadcasted_iota(I32, (n, n), d).astype(F32) for d in (0, 1))
    rank = ranks[...].reshape(1, n).astype(F32)
    order = orders[...].reshape(1, n).astype(F32)
    rank_down, order_down = turned(rank), turned(order)
    ahead = (rank_down > rank) | ((rank_down == rank) & (i < j))
    spot = jnp.sum(jnp.where(ahead, 1.0, 0.0), axis=0, keepdims=True)
    turn = sum(jnp.where(spot >= groups * m, 1.0, 0.0) for m in range(1, QUAD))
    k = spot - groups * turn
    back = (turn == 1.0) | (turn == 3.0)
    slot = QUAD * jnp.where(back, groups - 1.0 - k, k) + turn
    here = turned(slot) == j

    def dealt(values):
        return jnp.sum(jnp.where(here, values, 0.0), axis=0, keepdims=True)

    rank_here = dealt(rank_down)
    group, group_down = (sum(jnp.where(at >= QUAD * m, 1.0, 0.0) for m in range(1, groups)) for at in (j, i))
    rank_here_down = jnp.sum(jnp.where(slot == i, rank, 0.0), axis=1, keepdims=True)
    first = jnp.sum(jnp.where((group_down == group) & (i < j), rank_here_down, 0.0), axis=0, keepdims=True)
    for at, row in enumerate((dealt(i), first, rank_here, dealt(order_down))):
        plan[at:at + 1, :] = row.astype(I32)
    most = jnp.max(jnp.sum(jnp.where(group_down == group, rank_here_down, 0.0), axis=0, keepdims=True))
    pick[0] = sum((most > height).astype(I32) for height in heights[:-1])


def planned(heights, orders, ranks):
    vmem, smem = (pl.BlockSpec(memory_space=m) for m in (pltpu.VMEM, pltpu.SMEM))
    return pl.pallas_call(
        functools.partial(planning, heights),
        out_shape=(jax.ShapeDtypeStruct((4, ranks.shape[0]), I32), jax.ShapeDtypeStruct((1,), I32)),
        in_specs=[vmem, vmem],
        out_specs=(vmem, smem),
    )(orders, ranks)


def shards(coefficients, v_factors, transfer, u_factors, orders, ranks):
    most = QUAD * v_factors.shape[1]
    heights = tuple(most * part // 16 for part in PARTS)
    plan, pick = planned(heights, orders, ranks)

    def branch(rows, cid, plan, x, v, t, u):
        return dealt_out(plan, mixed(rows, cid, plan, x, v, t, u), x.shape)

    branches = [functools.partial(branch, rows, 1 + at) for at, rows in enumerate(heights)]
    return settled(lax.switch(pick[0], branches, plan, coefficients, v_factors, transfer, u_factors))


def solution(mesh):
    placed = (
        P(None, None, None, ("col", "rank")),
        P(None, None, ("col", "rank")),
        P(None, None, "col", None, None),
        P(None, None, ("col", "rank")),
        P(),
        P(),
    )
    return jax.shard_map(
        shards,
        mesh=mesh,
        in_specs=placed,
        out_specs=P(None, None, None, ("col", "rank")),
        check_vma=False,
    )
```
